32 devices in a mesh: member: 2 (over y), dom: 8 (over z, x), feat: 2 (over core).
Axes of the slice: x: 2, y: 2, z: 4, core: 2. Of those that a mesh axis runs over, the one named last changes fastest.
Arguments:
- grid_lat: bfloat16 [16384, 512], P(('member', 'dom'), 'feat'), parts along dimension 0, may hold values from -6 to 6
- mesh_lat: bfloat16 [8192, 512], P(('member', 'dom'), 'feat'), parts along dimension 0, may hold values from -6 to 6
- w_grid_send: bfloat16 [512, 512], P(None, 'feat'), may hold values from -0.25 to 0.25
- w_grid_recv: bfloat16 [512, 512], P(None, 'feat'), may hold values from -0.25 to 0.25
- g2m_bias: float32 [512], P('feat'), may hold values from -4 to 4
- w_grid_out: bfloat16 [512, 512], P('feat'), may hold values from -0.125 to 0.125
- w_edge_send: bfloat16 [512, 512], P(None, 'feat'), may hold values from -0.25 to 0.25
- w_edge_recv: bfloat16 [512, 512], P(None, 'feat'), may hold values from -0.25 to 0.25
- edge_bias: float32 [512], P('feat'), may hold values from -4 to 4
- w_edge_out: bfloat16 [512, 512], P('feat'), may hold values from -0.125 to 0.125
- send_grid: int32 [8, 4096], P('dom'), may hold values from 0 to 1023, as said below
- recv_row: int32 [8, 4096], P('dom'), may hold values from 0 to 512, as said below
- halo_rows: int32 [8, 1024], P('dom'), may hold values from 0 to 511, as said below
- edge_src: int32 [128, 128], P('dom'), may hold values from 0 to 1535, as said below
- edge_dst: int32 [128, 128], P('dom'), may hold values from 0 to 511
Outputs:
- mesh_encoded: bfloat16 [8192, 512], P(('member', 'dom'), 'feat'), parts along dimension 0
- mesh_out: bfloat16 [8192, 512], P(('member', 'dom'), 'feat'), parts along dimension 0
The draws below stay inside these ranges and needn't reach their ends.
There are 2 independent parts, one for each index of `member`. The reference program is written for one: setup_inputs(seed, part) draws one part's arguments, and reference() takes and returns one part's arrays. A program takes and returns all parts, laid end to end along the dimension named above; an argument that names none is the same for every part. Nothing has to cross between parts.
Inputs may be any that keep to these rules, and one draw needn't show every extreme that they name: `send_grid`: entry p, j * 512 + k names a grid row (within partition p) for slot k from p to j. Every grid row of p is named by exactly one slot whose recv_row entry is below 512. `recv_row`: entry j, p * 512 + k is the mesh row of partition j that slot k from p feeds, or 512 for an empty slot. In every draw some partition gets 512 filled slots from every partition. `halo_rows`: entry p, j * 128 + k is the k-th of 128 different mesh rows of partition p that partition j reads. `edge_src`: each value 512 to 1535 appears in every partition's tiles.
All inputs are finite; a program needn't handle non-finite values.
Results may differ from the reference program's by a relative error of at most 0.013.
Values may be sent and summed in bfloat16 or wider, within the bound.
No kernel may reach another device: no remote copies, remote signals or barrier semaphores. Data moves between devices by JAX's collectives and lax.ppermute only.
A program may use at most 64 MiB of HBM per device.

```python
import jax
import jax.numpy as jnp
from jax import lax

L = 512
H = 512
G_DEV = 1024
M_DEV = 512
HALO_ALL = 1024
TILES = 16
CAP = 512
HALO = 128
GRID = 8192
MESH = 4096
N_DOM = 8


def g2m_lists(key):
    hot_part = jax.random.randint(jax.random.fold_in(key, 5), (), 0, N_DOM).astype(jnp.int32)
    rest_count = G_DEV - CAP
    pool_index = jnp.arange((N_DOM - 1) * CAP, dtype=jnp.int32)
    pool_part = ((hot_part + 1 + pool_index // CAP) % N_DOM).astype(jnp.int32)

    def one_sender(sender_key):
        key_pool, key_order, key_rows = jax.random.split(sender_key, 3)
        picked = jax.random.permutation(key_pool, pool_part)[:rest_count]
        targets = jnp.concatenate([jnp.full((CAP,), hot_part, jnp.int32), picked.astype(jnp.int32)])
        grid_order = jax.random.permutation(key_order, G_DEV).astype(jnp.int32)
        mesh_dest = jax.random.randint(key_rows, (G_DEV,), 0, M_DEV).astype(jnp.int32)
        order = jnp.argsort(targets, stable=True)
        sorted_targets = targets[order]
        counts = jnp.sum((targets[None, :] == jnp.arange(N_DOM, dtype=jnp.int32)[:, None]).astype(jnp.int32), axis=1)
        starts = jnp.cumsum(counts) - counts
        position = (jnp.arange(G_DEV, dtype=jnp.int32) - starts[sorted_targets]).astype(jnp.int32)
        sending = jnp.zeros((N_DOM, CAP), jnp.int32).at[sorted_targets, position].set(grid_order[order])
        landing = jnp.full((N_DOM, CAP), M_DEV, jnp.int32).at[sorted_targets, position].set(mesh_dest[order])
        return (sending, landing)
    sender_keys = jax.random.split(jax.random.fold_in(key, 6), N_DOM)
    sending, landing = jax.vmap(one_sender)(sender_keys)
    send_lists = sending.reshape(N_DOM, N_DOM * CAP)
    recv_lists = jnp.transpose(landing, (1, 0, 2)).reshape(N_DOM, N_DOM * CAP)
    return (send_lists, recv_lists)


def edge_lists(key):
    edge_count = TILES * 128

    def one_part(part_key):
        key_cover, key_extra, key_dest, key_shuffle = jax.random.split(part_key, 4)
        cover = M_DEV + jax.random.permutation(key_cover, HALO_ALL).astype(jnp.int32)
        extra = jax.random.randint(key_extra, (edge_count - HALO_ALL,), 0, M_DEV + HALO_ALL).astype(jnp.int32)
        senders = jnp.concatenate([cover, extra])
        receivers = jax.random.randint(key_dest, (edge_count,), 0, M_DEV).astype(jnp.int32)
        shuffle = jax.random.permutation(key_shuffle, edge_count)
        return (senders[shuffle], receivers[shuffle])
    part_keys = jax.random.split(jax.random.fold_in(key, 8), N_DOM)
    senders, receivers = jax.vmap(one_part)(part_keys)
    return (senders.reshape(N_DOM * TILES, 128), receivers.reshape(N_DOM * TILES, 128))


def draw_send_grid(key, part):
    return g2m_lists(key)[0]


def draw_recv_row(key, part):
    return g2m_lists(key)[1]


def draw_halo_rows(key, part):
    key = jax.random.fold_in(key, 7)
    pair_keys = jax.random.split(key, N_DOM * N_DOM)
    chosen = jax.vmap(lambda pair_key: jax.random.permutation(pair_key, M_DEV)[:HALO])(pair_keys)
    return chosen.astype(jnp.int32).reshape(N_DOM, N_DOM * HALO)


def draw_edge_src(key, part):
    return edge_lists(key)[0]


def draw_edge_dst(key, part):
    return edge_lists(key)[1]


def block_scale(key, extent, shards, smallest, largest):
    factor_of, own = 1.0, jax.random.fold_in(key, 6)
    for axis_at, parts in shards:
        draws = jnp.exp(jax.random.uniform(jax.random.fold_in(own, axis_at), (parts,), jnp.float32, smallest / len(shards), largest / len(shards)))
        factor_of = factor_of * jnp.repeat(draws, extent[axis_at] // parts).reshape([-1 if axis == axis_at else 1 for axis in range(len(extent))])
    return factor_of


def normal_values(key, extent, scale, most, cuts=(), kind=jnp.bfloat16):
    result = scale * jax.random.normal(key, extent, jnp.float32)
    if cuts:
        result = result * block_scale(key, extent, cuts, -0.22, 0.18)
    return jnp.clip(result, -most, most).astype(kind)


def setup_inputs(seed: int = 0, part: int = 0) -> dict:
    splits = jax.random.split(jax.random.key(seed), 16)
    part_splits = jax.random.split(jax.random.fold_in(splits[15], part), 16)
    return {
        "grid_lat": normal_values(part_splits[0], (GRID, L), 1.0, 6.0, ((0, 8), (1, 2))),
        "mesh_lat": normal_values(part_splits[1], (MESH, L), 1.0, 6.0, ((0, 8), (1, 2))),
        "w_grid_send": normal_values(splits[2], (L, H), L ** -0.5, 0.25, ((1, 2),)),
        "w_grid_recv": normal_values(splits[3], (L, H), L ** -0.5, 0.25, ((1, 2),)),
        "g2m_bias": normal_values(splits[4], (H,), 1.0, 4.0, ((0, 2),), jnp.float32),
        "w_grid_out": normal_values(splits[5], (H, L), (4 * H) ** -0.5, 0.125, ((0, 2),)),
        "w_edge_send": normal_values(splits[6], (L, H), L ** -0.5, 0.25, ((1, 2),)),
        "w_edge_recv": normal_values(splits[7], (L, H), L ** -0.5, 0.25, ((1, 2),)),
        "edge_bias": normal_values(splits[8], (H,), 1.0, 4.0, ((0, 2),), jnp.float32),
        "w_edge_out": normal_values(splits[9], (H, L), (H * TILES * 128 // M_DEV) ** -0.5, 0.125, ((0, 2),)),
        "send_grid": draw_send_grid(jax.random.fold_in(splits[15], 71), part),
        "recv_row": draw_recv_row(jax.random.fold_in(splits[15], 71), part),
        "halo_rows": draw_halo_rows(jax.random.fold_in(splits[15], 71), part),
        "edge_src": draw_edge_src(jax.random.fold_in(splits[15], 71), part),
        "edge_dst": draw_edge_dst(jax.random.fold_in(splits[15], 71), part),
    }


def reference(grid_lat, mesh_lat, w_grid_send, w_grid_recv, g2m_bias, w_grid_out, w_edge_send, w_edge_recv, edge_bias, w_edge_out, send_grid, recv_row, halo_rows, edge_src, edge_dst):
    grid_proj = jnp.dot(grid_lat, w_grid_send, preferred_element_type=jnp.float32).astype(jnp.bfloat16)
    mesh_rproj = jnp.dot(mesh_lat, w_grid_recv, preferred_element_type=jnp.float32).astype(jnp.bfloat16)
    send_table = send_grid.reshape(N_DOM, N_DOM, CAP)
    source_base = (jnp.arange(N_DOM, dtype=jnp.int32) * G_DEV)[:, None]

    def g2m_part(part_index):
        grid_ids = (send_table[:, part_index, :] + source_base).reshape(-1).astype(jnp.int32)
        dest_rows = recv_row[part_index]
        mesh_block = lax.dynamic_slice_in_dim(mesh_rproj, (part_index * M_DEV).astype(jnp.int32), M_DEV, 0)
        mesh_term = jnp.take(mesh_block, dest_rows, axis=0, mode="clip")
        preact = grid_proj[grid_ids].astype(jnp.float32) + mesh_term.astype(jnp.float32) + g2m_bias.astype(jnp.float32)
        hidden = jax.nn.silu(preact).astype(jnp.bfloat16)
        summed = jax.ops.segment_sum(hidden.astype(jnp.float32), dest_rows, num_segments=M_DEV + 1)[:M_DEV]
        return summed.astype(jnp.bfloat16)

    g2m_sum = lax.map(g2m_part, jnp.arange(N_DOM, dtype=jnp.int32)).reshape(N_DOM * M_DEV, H)
    mesh_encoded = (mesh_lat.astype(jnp.float32) + jnp.dot(g2m_sum, w_grid_out, preferred_element_type=jnp.float32)).astype(jnp.bfloat16)
    send_proj = jnp.dot(mesh_encoded, w_edge_send, preferred_element_type=jnp.float32).astype(jnp.bfloat16)
    recv_proj = jnp.dot(mesh_encoded, w_edge_recv, preferred_element_type=jnp.float32).astype(jnp.bfloat16)
    sender_all = edge_src.reshape(N_DOM, TILES * 128)
    receiver_all = edge_dst.reshape(N_DOM, TILES * 128)

    def proc_part(part_index):
        senders = sender_all[part_index]
        receivers = receiver_all[part_index]
        halo_slot = jnp.maximum(senders - M_DEV, 0).astype(jnp.int32)
        owner_part = (halo_slot // HALO).astype(jnp.int32)
        lookup = halo_rows[owner_part, part_index * HALO + halo_slot % HALO]
        global_ids = jnp.where(senders < M_DEV, part_index * M_DEV + senders, owner_part * M_DEV + lookup).astype(jnp.int32)
        recv_block = lax.dynamic_slice_in_dim(recv_proj, (part_index * M_DEV).astype(jnp.int32), M_DEV, 0)
        preact = send_proj[global_ids].astype(jnp.float32) + recv_block[receivers].astype(jnp.float32) + edge_bias.astype(jnp.float32)
        hidden = jax.nn.silu(preact).astype(jnp.bfloat16)
        summed = jax.ops.segment_sum(hidden.astype(jnp.float32), receivers, num_segments=M_DEV)
        return summed.astype(jnp.bfloat16)

    proc_sum = lax.map(proc_part, jnp.arange(N_DOM, dtype=jnp.int32)).reshape(N_DOM * M_DEV, H)
    mesh_out = (mesh_encoded.astype(jnp.float32) + jnp.dot(proc_sum, w_edge_out, preferred_element_type=jnp.float32)).astype(jnp.bfloat16)
    return mesh_encoded, mesh_out
```

```python
import jax
import jax.numpy as jnp
from jax import lax
from jax.sharding import PartitionSpec as P

BF16, F32 = jnp.bfloat16, jnp.float32


def dot(a, b):
    return jnp.dot(a, b, preferred_element_type=F32)


def hot_rows(index, width):
    return (index[:, None] == lax.broadcasted_iota(jnp.int32, (index.shape[0], width), 1)).astype(BF16)


def hot_columns(index, height):
    return (lax.broadcasted_iota(jnp.int32, (height, index.shape[0]), 0) == index[None, :]).astype(BF16)


def swap(x):
    return lax.ppermute(x, "feat", [(0, 1), (1, 0)])


def from_xor(x, bits, n_dom):
    return lax.ppermute(x, "dom", [(i, i ^ bits) for i in range(n_dom)])


def own_first(w, axis):
    return jnp.where(lax.axis_index("feat") == 0, w, jnp.roll(w, w.shape[axis] // 2, axis))


def silu_bf16(v):
    return (v / (1.0 + jnp.exp(-v))).astype(BF16)


def block(row, at, size):
    return lax.dynamic_slice_in_dim(row, at * size, size, 0)


def sums_by_halves(grid_proj, mesh_rproj, bias, send_grid, recv_row, n_dom):
    me = lax.axis_index("dom")
    half = n_dom // 2
    mesh_rows = mesh_rproj.shape[0]
    grid_rows = grid_proj.shape[0]
    cap = send_grid.shape[0] // n_dom
    width = grid_proj.shape[1] // 2
    send_mirror = from_xor(send_grid, half, n_dom)
    recv_near = [recv_row] + [from_xor(recv_row, k, n_dom) for k in range(1, half)]
    mirrored = [from_xor(grid_proj[:, c * width : (c + 1) * width], half, n_dom) for c in range(2)]
    table = jnp.concatenate([mesh_rproj] + [from_xor(mesh_rproj, k, n_dom) for k in range(1, half)], axis=0)

    def targets_of(sender, send_list):
        ids = jnp.concatenate([block(send_list, me ^ k, cap) for k in range(half)])
        rows = [block(recv_near[k], sender, cap) for k in range(half)]
        goal = jnp.concatenate([jnp.where(r < mesh_rows, r + (k * mesh_rows + 1), 0) for k, r in enumerate(rows)])
        match = lax.broadcasted_iota(jnp.int32, (grid_rows, ids.shape[0]), 0) == ids[None, :]
        return jnp.sum(jnp.where(match, goal[None, :], 0), axis=1) - 1

    goal_own = targets_of(me, send_grid)
    goal_mirror = targets_of(me ^ half, send_mirror)
    term_own = dot(hot_rows(goal_own, half * mesh_rows), table) + bias[None, :]
    term_mirror = dot(hot_rows(goal_mirror, half * mesh_rows), table) + bias[None, :]
    hidden_own = silu_bf16(grid_proj.astype(F32) + term_own)
    sum_own = dot(hot_columns(goal_own, half * mesh_rows), hidden_own)
    chunks = []
    for c in range(2):
        part = slice(c * width, (c + 1) * width)
        hidden = silu_bf16(mirrored[c].astype(F32) + term_mirror[:, part])
        total = sum_own[:, part] + dot(hot_columns(goal_mirror, half * mesh_rows), hidden)
        result = total[:mesh_rows]
        for k in range(1, half):
            result += from_xor(total[k * mesh_rows : (k + 1) * mesh_rows].astype(BF16), k, n_dom).astype(F32)
        chunks.append(result.astype(BF16))
    return chunks


def sums_by_all_to_all(grid_proj, mesh_rproj, bias, send_grid, recv_row, n_dom):
    packed = dot(hot_rows(send_grid, grid_proj.shape[0]), grid_proj).astype(BF16)
    arrived = lax.all_to_all(packed, "dom", split_axis=0, concat_axis=0, tiled=True)
    term = dot(hot_rows(recv_row, mesh_rproj.shape[0]), mesh_rproj) + bias[None, :]
    hidden = silu_bf16(arrived.astype(F32) + term)
    return [dot(hot_columns(recv_row, mesh_rproj.shape[0]), hidden).astype(BF16)]


def shards(
    grid_lat,
    mesh_lat,
    w_grid_send,
    w_grid_recv,
    g2m_bias,
    w_grid_out,
    w_edge_send,
    w_edge_recv,
    edge_bias,
    w_edge_out,
    send_grid,
    recv_row,
    halo_rows,
    edge_src,
    edge_dst,
):
    n_dom = lax.axis_size("dom")
    mesh_rows, feats = mesh_lat.shape
    grid_other = swap(grid_lat)
    mesh_other = swap(mesh_lat)
    w_send = own_first(w_grid_send, 0)
    w_recv = own_first(w_grid_recv, 0)
    grid_proj = (dot(grid_lat, w_send[:feats]) + dot(grid_other, w_send[feats:])).astype(BF16)
    mesh_rproj = (dot(mesh_lat, w_recv[:feats]) + dot(mesh_other, w_recv[feats:])).astype(BF16)
    w_out = own_first(w_grid_out, 1)
    w_out_other = own_first(swap(w_grid_out), 1)
    w_out2 = w_edge_out[:, :]
    w_out2_other = swap(w_edge_out)
    own_at = lax.axis_index("feat") * feats
    w_out2 = lax.dynamic_slice_in_dim(w_out2, own_at, feats, 1)
    w_out2_other = lax.dynamic_slice_in_dim(w_out2_other, own_at, feats, 1)
    w_edge = jnp.concatenate([own_first(w_edge_send, 0), own_first(w_edge_recv, 0)], axis=1)

    sums = sums_by_halves if n_dom == 8 else sums_by_all_to_all
    chunks = sums(grid_proj, mesh_rproj, g2m_bias, send_grid.reshape(-1), recv_row.reshape(-1), n_dom)

    update = jnp.zeros((mesh_rows, 2 * feats), F32)
    at = 0
    for chunk in chunks:
        rows = slice(at, at + chunk.shape[1])
        update += dot(chunk, w_out[rows]) + dot(swap(chunk), w_out_other[rows])
        at += chunk.shape[1]
    encoded = (jnp.concatenate([mesh_lat, mesh_other], axis=1).astype(F32) + update).astype(BF16)
    mesh_encoded = encoded[:, :feats]

    proj = dot(encoded, w_edge).astype(BF16)
    send_proj, recv_proj = proj[:, :feats], proj[:, feats:]
    halo_out = dot(hot_rows(halo_rows.reshape(-1), mesh_rows), send_proj).astype(BF16)
    halo_in = lax.all_to_all(halo_out, "dom", split_axis=0, concat_axis=0, tiled=True)

    senders = edge_src.reshape(-1)
    receivers = edge_dst.reshape(-1)
    near = (
        dot(hot_rows(senders, mesh_rows), send_proj)
        + dot(hot_rows(receivers, mesh_rows), recv_proj)
        + edge_bias[None, :]
    )
    far = dot(hot_rows(senders - mesh_rows, halo_in.shape[0]), halo_in)
    hidden = silu_bf16(near + far)
    proc_sum = dot(hot_columns(receivers, mesh_rows), hidden).astype(BF16)
    update = dot(proc_sum, w_out2) + dot(swap(proc_sum), w_out2_other)
    mesh_out = (mesh_encoded.astype(F32) + update).astype(BF16)
    return (mesh_encoded, mesh_out)


def solution(mesh):
    placed = (
        P(("member", "dom"), "feat"),
        P(("member", "dom"), "feat"),
        P(None, "feat"),
        P(None, "feat"),
        P("feat"),
        P("feat", None),
        P(None, "feat"),
        P(None, "feat"),
        P("feat"),
        P("feat", None),
        P("dom", None),
        P("dom", None),
        P("dom", None),
        P("dom", None),
        P("dom", None),
    )
    return jax.shard_map(
        shards,
        mesh=mesh,
        in_specs=placed,
        out_specs=(P(("member", "dom"), "feat"), P(("member", "dom"), "feat")),
        check_vma=False,
    )
```

```python
import functools

import jax
import jax.numpy as jnp
from jax import lax
from jax.experimental import pallas as pl
from jax.experimental.pallas import tpu as pltpu
from jax.sharding import PartitionSpec as P

BF16, F32, I32 = jnp.bfloat16, jnp.float32, jnp.int32
LANES = 128
STEP = 256
SMEM = pl.BlockSpec(memory_space=pltpu.SMEM)
VMEM = pl.BlockSpec(memory_space=pltpu.VMEM)
HBM = pl.BlockSpec(memory_space=pltpu.HBM)


def dot(a, b):
    return jnp.dot(a, b, preferred_element_type=F32)


def iota(shape, axis):
    return lax.broadcasted_iota(I32, shape, axis)


def silu_bf16(v):
    return (v / (1.0 + jnp.exp(-v))).astype(BF16)


def shape_of(shape, dtype):
    return jax.ShapeDtypeStruct(shape, dtype)


def position(axis):
    return lax.axis_index(axis).astype(I32).reshape(1)


def swap(x):
    return lax.ppermute(x, "feat", [(0, 1), (1, 0)])


def from_xor(x, bits, n_dom):
    return lax.ppermute(x, "dom", [(i, i ^ bits) for i in range(n_dom)])


def call(kernel, out_shape, *args, specs=None, outs=None, name, scratch=(), mib=32):
    return pl.pallas_call(
        kernel,
        out_shape=out_shape,
        in_specs=[VMEM] * len(args) if specs is None else specs,
        out_specs=jax.tree.map(lambda _: VMEM, out_shape) if outs is None else outs,
        scratch_shapes=scratch,
        compiler_params=pltpu.CompilerParams(vmem_limit_bytes=mib << 20),
        name=name,
    )(*args)


def halves_of(feat, size):
    own = pl.ds(pl.multiple_of(feat * size, size), size)
    other = pl.ds(pl.multiple_of((1 - feat) * size, size), size)
    return own, other


def fetch_lists(send_list, recv_list, n_dom):
    near, far = (1, 3), (2, 4)
    fetched = []
    for step in range(2):
        what = jnp.where(lax.axis_index("feat") == 1, send_list, recv_list) if step else recv_list
        pairs = [(2 * d, 2 * (d ^ near[step])) for d in range(n_dom)]
        pairs += [(2 * d + 1, 2 * (d ^ far[step]) + 1) for d in range(n_dom)]
        fetched.append(lax.ppermute(what, ("dom", "feat"), pairs))
    return jnp.concatenate(fetched, axis=1)


def start_copies(source, target, sems, first, pieces):
    rows = source.shape[0] // pieces
    copies = []
    for n in range(pieces):
        part = pl.ds(n * rows, rows)
        copies.append(pltpu.make_async_copy(source.at[part], target.at[part], sems.at[first + n]))
        copies[-1].start()
    return copies


def wait_copies(copies):
    for copy in copies:
        copy.wait()


def own_features_kernel(feat, grid, mesh, w_send, w_recv, grid_part, mesh_part, send_rest, recv_rest, *scratch):
    ws, g, wr, m, sems = scratch
    first = start_copies(w_send, ws, sems, 0, 4) + start_copies(grid, g, sems, 4, 4)
    second = start_copies(w_recv, wr, sems, 8, 4) + start_copies(mesh, m, sems, 12, 4)
    own, other = halves_of(feat[0], g.shape[1])
    wait_copies(first)
    grid_part[...] = dot(g[...], ws[own, :])
    send_rest[...] = ws[other, :]
    wait_copies(second)
    mesh_part[...] = dot(m[...], wr[own, :])
    recv_rest[...] = wr[other, :]


def other_features_kernel(part, rest, other, *outs):
    width = outs[0].shape[1]
    for c, out in enumerate(outs):
        lanes = slice(c * width, (c + 1) * width)
        out[...] = (part[:, lanes] + dot(other[...], rest[:, lanes])).astype(BF16)


def project(grid, mesh, w_send, w_recv, n_chunks):
    grid_other, mesh_other = swap(grid), swap(mesh)
    hidden, feats = w_send.shape[1], grid.shape[1]
    parts = call(
        own_features_kernel,
        [
            shape_of((grid.shape[0], hidden), F32),
            shape_of((mesh.shape[0], hidden), F32),
            shape_of((feats, hidden), BF16),
            shape_of((feats, hidden), BF16),
        ],
        position("feat"),
        *[pltpu.with_memory_space_constraint(x, pltpu.HBM) for x in (grid, mesh, w_send, w_recv)],
        specs=[SMEM] + [HBM] * 4,
        scratch=[pltpu.VMEM(x.shape, BF16) for x in (w_send, grid, w_recv, mesh)] + [pltpu.SemaphoreType.DMA((16,))],
        name="own_features",
        mib=16,
    )
    grid_part, mesh_part, send_rest, recv_rest = parts
    chunk = shape_of((grid.shape[0], hidden // n_chunks), BF16)
    chunks = call(
        other_features_kernel, [chunk] * n_chunks, grid_part, send_rest, grid_other, name="other_grid_features"
    )
    chunks, mesh_part = lax.optimization_barrier((chunks, mesh_part))
    (mesh_proj,) = call(
        other_features_kernel,
        [shape_of((mesh.shape[0], hidden), BF16)],
        mesh_part,
        recv_rest,
        mesh_other,
        name="other_mesh_features",
    )
    return chunks, mesh_proj, mesh_other


def across(row):
    return jnp.transpose(jnp.broadcast_to(row.astype(F32), (LANES, LANES))).astype(I32)


def goals_kernel(half, mesh_rows, me, feat, send_own, recv_own, mine, other, *outs):
    size = send_own.shape[1]
    cap = size // (2 * half)
    blocks = outs[0].shape[0] // LANES
    digit = 64

    def pick(from_second, step, block):
        at = pl.ds(pl.multiple_of(step * size + block * cap, cap), cap)
        return jnp.where(feat[0] == from_second, mine[:, at], other[:, at])

    def block(ref, n):
        return ref[:, pl.ds(pl.multiple_of(n * cap, cap), cap)]

    for sender, column, row in ((me[0], outs[0], outs[1]), (me[0] ^ half, outs[2], outs[3])):
        rows = (block(recv_own, sender), pick(0, 0, sender), pick(1, 0, sender), pick(0, 1, sender))
        ids = [block(send_own, me[0] ^ k) if column is outs[0] else pick(1, 1, me[0] ^ k) for k in range(half)]
        values = [jnp.where(r < mesh_rows, r + (k * mesh_rows + 1), 0) for k, r in enumerate(rows)]
        ids, values = jnp.concatenate(ids, axis=1), jnp.concatenate(values, axis=1)
        into_block = iota((blocks, ids.shape[1]), 0) == ids // LANES
        into_lane = (iota((LANES, ids.shape[1]), 0) == ids % LANES).astype(BF16)
        goal = jnp.full((blocks, LANES), -1.0, F32)
        for scale, part in ((digit, values // digit), (1, values % digit)):
            entries = jnp.where(into_block, part, 0).astype(F32).astype(BF16)
            goal += scale * lax.dot_general(entries, into_lane, (((1,), (1,)), ((), ())), preferred_element_type=F32)
        for b in range(blocks):
            part = slice(b * LANES, (b + 1) * LANES)
            found = goal[b : b + 1, :]
            column[part, :] = across(found)
            row[:, part] = jnp.broadcast_to(found, (row.shape[0], LANES)).astype(I32)


def add_terms(term, goal, tables, first):
    for k, table in enumerate(tables):
        hot = goal == iota((goal.shape[0], table.shape[0]), 1) + (first + k) * table.shape[0]
        term += dot(hot.astype(BF16), table[...])
    return term


def terms_kernel(first, n_tables, *refs):
    start_own, start_mirror, goal_own, goal_mirror, *tables = refs[: 4 + n_tables]
    for start, goal, out in zip((start_own, start_mirror), (goal_own, goal_mirror), refs[4 + n_tables :]):

        @pl.loop(0, out.shape[0] // STEP)
        def _(i):
            at = pl.ds(pl.multiple_of(i * STEP, STEP), STEP)
            begin = jnp.broadcast_to(start[...], (STEP, out.shape[1])) if start.shape[0] == 1 else start[at, :]
            out[at, :] = add_terms(begin, goal[at, :][:, :1], tables, first)


def own_sums_kernel(half, term_own, term_mirror, goal_own, goal_mirror, row_own, table, g0, g1, sums, mirror_out, hidden):
    grid_rows, width = g0.shape

    @pl.loop(0, grid_rows // STEP)
    def _(i):
        at = pl.ds(pl.multiple_of(i * STEP, STEP), STEP)
        mirror_out[at, :] = add_terms(term_mirror[at, :], goal_mirror[at, :][:, :1], (table,), half - 1)
        term = add_terms(term_own[at, :], goal_own[at, :][:, :1], (table,), half - 1)
        for c, g in enumerate((g0, g1)):
            part = slice(c * width, (c + 1) * width)
            hidden[at, part] = silu_bf16(g[at, :].astype(F32) + term[:, part])

    goal = row_own[:1, :]

    @pl.loop(0, sums.shape[0] // STEP)
    def _(i):
        hot = iota((STEP, grid_rows), 0) + i * STEP == goal
        sums[pl.ds(pl.multiple_of(i * STEP, STEP), STEP), :] = dot(hot.astype(BF16), hidden[...])


def far_sums_kernel(chunk, mirrored, term, row, sums, *outs):
    width = mirrored.shape[1]
    part = slice(chunk * width, (chunk + 1) * width)
    hidden = silu_bf16(mirrored[...].astype(F32) + term[:, part])
    goal = row[:1, :]
    for k, out in enumerate(outs):
        for at in range(0, out.shape[0], STEP):
            first = k * out.shape[0] + at
            hot = iota((STEP, goal.shape[1]), 0) + first == goal
            total = sums[first : first + STEP, part] + dot(hot.astype(BF16), hidden)
            out[at : at + STEP, :] = total.astype(out.dtype)


def sums_by_halves(grid_chunks, mesh_rproj, bias, send_grid, recv_row, fetched, n_dom):
    half = n_dom // 2
    mesh_rows, hidden = mesh_rproj.shape
    grid_rows, width = grid_chunks[0].shape
    tables = [mesh_rproj] + [from_xor(mesh_rproj, k, n_dom) for k in range(1, half)]
    mirrored = [from_xor(grid_chunks[0], half, n_dom)]
    fetched, later = lax.optimization_barrier((fetched, grid_chunks[1]))
    mirrored.append(from_xor(later, half, n_dom))
    column, row = shape_of((grid_rows, LANES), I32), shape_of((8, grid_rows), I32)
    goal_own, row_own, goal_mirror, row_mirror = call(
        functools.partial(goals_kernel, half, mesh_rows),
        [column, row, column, row],
        position("dom"),
        position("feat"),
        send_grid,
        recv_row,
        fetched,
        swap(fetched),
        specs=[SMEM] * 2 + [VMEM] * 4,
        name="goals",
    )
    term = shape_of((grid_rows, hidden), F32)
    terms = (bias[None, :], bias[None, :])
    for first, some in ((0, tables[:2]), (2, tables[2:3])):
        terms = call(
            functools.partial(terms_kernel, first, len(some)),
            [term, term],
            *terms,
            goal_own,
            goal_mirror,
            *some,
            name="mesh_terms",
        )
    sums, term_mirror = call(
        functools.partial(own_sums_kernel, half),
        [shape_of((half * mesh_rows, hidden), F32), term],
        *terms,
        goal_own,
        goal_mirror,
        row_own,
        tables[3],
        *grid_chunks,
        scratch=[pltpu.VMEM((grid_rows, hidden), BF16)],
        name="own_sums",
    )
    chunks = []
    for c in range(2):
        parts = call(
            functools.partial(far_sums_kernel, c),
            [shape_of((mesh_rows, width), BF16 if k else F32) for k in range(half)],
            mirrored[c],
            term_mirror,
            row_mirror,
            sums,
            name="far_sums",
        )
        result = parts[0]
        for k in range(1, half):
            result += from_xor(parts[k], k, n_dom).astype(F32)
        chunks.append(result.astype(BF16))
    return chunks


def sums_by_all_to_all(grid_chunks, mesh_rproj, bias, send_grid, recv_row, fetched, n_dom):
    def rows_of(table, index):
        hot = index[0][:, None] == iota((index.shape[1], table.shape[0]), 1)
        return dot(hot.astype(BF16), table)

    packed = rows_of(grid_chunks[0], send_grid).astype(BF16)
    arrived = lax.all_to_all(packed, "dom", split_axis=0, concat_axis=0, tiled=True)
    hidden = silu_bf16(arrived.astype(F32) + rows_of(mesh_rproj, recv_row) + bias[None, :])
    into = iota((mesh_rproj.shape[0], recv_row.shape[1]), 0) == recv_row
    return [dot(into.astype(BF16), hidden).astype(BF16)]


def encode_kernel(n_chunks, feat, *refs):
    chunks, others = refs[:n_chunks], refs[n_chunks : 2 * n_chunks]
    w_own, w_other, mesh_own, mesh_other, w_send, halo_rows = refs[2 * n_chunks : 2 * n_chunks + 6]
    full_out, send_out, halo_out, update, full, send_proj, halo, sem = refs[2 * n_chunks + 6 :]
    width, feats = chunks[0].shape[1], mesh_own.shape[1]
    total = 0.0
    for c, (mine, other) in enumerate(zip(chunks, others)):
        rows = slice(c * width, (c + 1) * width)
        total += dot(mine[...], w_own[rows, :]) + dot(other[...], w_other[rows, :])
    update[...] = total
    own, rest = halves_of(feat[0], feats)
    full[:, own] = (mesh_own[...].astype(F32) + update[:, own]).astype(BF16)
    full[:, rest] = (mesh_other[...].astype(F32) + update[:, rest]).astype(BF16)
    sent = start_copies(full, full_out, sem, 0, 2)
    send_proj[...] = dot(full[...], w_send[...]).astype(BF16)
    sent += start_copies(send_proj, send_out, sem, 2, 1)
    for at in range(0, halo.shape[0], LANES):
        rows = slice(at, at + LANES)
        hot = across(halo_rows[:, rows])[:, :1] == iota((LANES, send_proj.shape[0]), 1)
        halo[rows, :] = dot(hot.astype(BF16), send_proj[...]).astype(BF16)
        if rows.stop % STEP == 0:
            done = slice(rows.stop - STEP, rows.stop)
            sent.append(pltpu.make_async_copy(halo.at[done], halo_out.at[done], sem.at[len(sent)]))
            sent[-1].start()
    wait_copies(sent)


def near_edges_kernel(feat, full, send_proj, w_recv, bias, src, dst, w_own, w_other, near, src_at, dst_row, w_out, encoded):
    feats = encoded.shape[1]
    own, _ = halves_of(feat[0], feats)
    encoded[...] = full[:, own]
    recv_proj = dot(full[...], w_recv[...]).astype(BF16)
    for b in range(src.shape[0]):
        rows = slice(b * LANES, (b + 1) * LANES)
        src_at[rows, :] = across(src[b : b + 1, :])
        dst_row[:, rows] = dst[b : b + 1, :]
        dst_at = across(dst[b : b + 1, :])[:, :1]
        term = dot((src_at[rows, :1] == iota((LANES, send_proj.shape[0]), 1)).astype(BF16), send_proj[...])
        term += dot((dst_at == iota((LANES, send_proj.shape[0]), 1)).astype(BF16), recv_proj)
        near[rows, :] = term + bias[...]
    w_out[: w_own.shape[0], :] = w_own[:, own]
    w_out[w_own.shape[0] :, :] = w_other[:, own]


def edge_sums_kernel(halo_rows, near, src_at, dst_row, out, halo, sem):
    arrival = start_copies(halo_rows, halo, sem, 0, 8)
    mesh_rows = out.shape[0]
    total = jnp.zeros(out.shape, F32)
    wait_copies(arrival)
    for at in range(0, near.shape[0], STEP):
        rows = slice(at, at + STEP)
        hot = src_at[rows, :1] - mesh_rows == iota((STEP, halo.shape[0]), 1)
        hidden = silu_bf16(near[rows, :] + dot(hot.astype(BF16), halo[...]))
        into = iota((mesh_rows, STEP), 0) == dst_row[:, rows]
        total += dot(into.astype(BF16), hidden)
    out[...] = total.astype(BF16)


def output_kernel(encoded, mine, other, w_out, out):
    hidden = mine.shape[1]
    update = dot(mine[...], w_out[:hidden, :]) + dot(other[...], w_out[hidden:, :])
    out[...] = (encoded[...].astype(F32) + update).astype(BF16)


def shards(
    grid_lat,
    mesh_lat,
    w_grid_send,
    w_grid_recv,
    g2m_bias,
    w_grid_out,
    w_edge_send,
    w_edge_recv,
    edge_bias,
    w_edge_out,
    send_grid,
    recv_row,
    halo_rows,
    edge_src,
    edge_dst,
):
    n_dom = lax.axis_size("dom")
    mesh_rows, feats = mesh_lat.shape
    hidden = w_grid_send.shape[1]
    halves = n_dom == 8
    grid_chunks, mesh_rproj, mesh_other = project(grid_lat, mesh_lat, w_grid_send, w_grid_recv, 2 if halves else 1)
    grid_chunks, mesh_rproj, send_grid, recv_row, w_grid_out, w_edge_out = lax.optimization_barrier(
        (grid_chunks, mesh_rproj, send_grid, recv_row, w_grid_out, w_edge_out)
    )
    fetched = fetch_lists(send_grid, recv_row, n_dom) if halves else None
    sums = sums_by_halves if halves else sums_by_all_to_all
    chunks = sums(grid_chunks, mesh_rproj, g2m_bias, send_grid, recv_row, fetched, n_dom)

    feat = position("feat")
    full, send_proj, halo_out = call(
        functools.partial(encode_kernel, len(chunks)),
        [
            pltpu.HBM((mesh_rows, 2 * feats), BF16),
            pltpu.HBM((mesh_rows, hidden), BF16),
            pltpu.HBM((halo_rows.shape[1], hidden), BF16),
        ],
        feat,
        *chunks,
        *[swap(chunk) for chunk in chunks],
        w_grid_out,
        swap(w_grid_out),
        mesh_lat,
        mesh_other,
        w_edge_send,
        halo_rows,
        specs=[SMEM] + [VMEM] * (2 * len(chunks) + 6),
        scratch=[
            pltpu.VMEM((mesh_rows, 2 * feats), F32),
            pltpu.VMEM((mesh_rows, 2 * feats), BF16),
            pltpu.VMEM((mesh_rows, hidden), BF16),
            pltpu.VMEM((halo_rows.shape[1], hidden), BF16),
            pltpu.SemaphoreType.DMA((3 + halo_rows.shape[1] // STEP,)),
        ],
        outs=[HBM] * 3,
        name="encode",
    )
    halo_in = lax.all_to_all(halo_out, "dom", split_axis=0, concat_axis=0, tiled=True)
    edges = edge_src.shape[0] * edge_src.shape[1]
    near, src_at, dst_row, w_out, mesh_encoded = call(
        near_edges_kernel,
        [
            shape_of((edges, hidden), F32),
            shape_of((edges, LANES), I32),
            shape_of((1, edges), I32),
            shape_of((2 * w_edge_out.shape[0], feats), BF16),
            shape_of((mesh_rows, feats), BF16),
        ],
        feat,
        full,
        send_proj,
        w_edge_recv,
        edge_bias[None, :],
        edge_src,
        edge_dst,
        w_edge_out,
        swap(w_edge_out),
        specs=[SMEM] + [VMEM] * 8,
        name="near_edges",
    )
    proc_sum = call(
        edge_sums_kernel,
        shape_of((mesh_rows, hidden), BF16),
        pltpu.with_memory_space_constraint(halo_in, pltpu.HBM),
        near,
        src_at,
        dst_row,
        specs=[HBM] + [VMEM] * 3,
        scratch=[pltpu.VMEM(halo_in.shape, BF16), pltpu.SemaphoreType.DMA((8,))],
        name="edge_sums",
    )
    mesh_out = call(
        output_kernel,
        shape_of((mesh_rows, feats), BF16),
        mesh_encoded,
        proc_sum,
        swap(proc_sum),
        w_out,
        name="output",
    )
    return (mesh_encoded, mesh_out)


def solution(mesh):
    rows = P(("member", "dom"), "feat")
    columns, lists = P(None, "feat"), P("dom", None)
    placed = (rows, rows, columns, columns, P("feat"), P("feat", None), columns, columns, P("feat"), P("feat", None))
    return jax.shard_map(
        shards,
        mesh=mesh,
        in_specs=placed + (lists,) * 5,
        out_specs=(rows, rows),
        check_vma=False,
    )
```

```python
import functools

import jax
import jax.numpy as jnp
from jax import lax
from jax.experimental import pallas as pl
from jax.experimental.pallas import tpu as pltpu
from jax.sharding import PartitionSpec as P

BF16, F32, I32 = jnp.bfloat16, jnp.float32, jnp.int32
LANES = 128
STEP = 256
MIB = 24
SMEM = pl.BlockSpec(memory_space=pltpu.SMEM)
VMEM = pl.BlockSpec(memory_space=pltpu.VMEM)
HBM = pl.BlockSpec(memory_space=pltpu.HBM)


def dot(a, b):
    return jnp.dot(a, b, preferred_element_type=F32)


def iota(shape, axis):
    return lax.broadcasted_iota(I32, shape, axis)


def silu_bf16(v):
    return (v / (1.0 + jnp.exp(-v))).astype(BF16)


def shape_of(shape, dtype):
    return jax.ShapeDtypeStruct(shape, dtype)


def position(axis):
    return lax.axis_index(axis).astype(I32).reshape(1)


def swap(x):
    return lax.ppermute(x, "feat", [(0, 1), (1, 0)])


def from_xor(x, bits, n_dom):
    return lax.ppermute(x, "dom", [(i, i ^ bits) for i in range(n_dom)])


def call(kernel, out_shape, *args, specs=None, outs=None, name, scratch=(), mib=MIB):
    return pl.pallas_call(
        kernel,
        out_shape=out_shape,
        in_specs=[VMEM] * len(args) if specs is None else specs,
        out_specs=jax.tree.map(lambda _: VMEM, out_shape) if outs is None else outs,
        scratch_shapes=scratch,
        compiler_params=pltpu.CompilerParams(vmem_limit_bytes=mib << 20),
        name=name,
    )(*args)


def halves_of(feat, size):
    own = pl.ds(pl.multiple_of(feat * size, size), size)
    other = pl.ds(pl.multiple_of((1 - feat) * size, size), size)
    return own, other


def start_copies(source, target, sems, first, pieces):
    rows = source.shape[0] // pieces
    copies = []
    for n in range(pieces):
        part = pl.ds(n * rows, rows)
        copies.append(pltpu.make_async_copy(source.at[part], target.at[part], sems.at[first + n]))
        copies[-1].start()
    return copies


def wait_copies(copies):
    for copy in copies:
        copy.wait()


def own_features_kernel(feat, grid, mesh, w_send, w_recv, grid_part, mesh_part, send_rest, recv_rest, *scratch):
    ws, g, wr, m, sems = scratch
    first = start_copies(w_send, ws, sems, 0, 4) + start_copies(grid, g, sems, 4, 4)
    second = start_copies(w_recv, wr, sems, 8, 4) + start_copies(mesh, m, sems, 12, 4)
    own, other = halves_of(feat[0], g.shape[1])
    wait_copies(first)
    grid_part[...] = dot(g[...], ws[own, :])
    send_rest[...] = ws[other, :]
    wait_copies(second)
    mesh_part[...] = dot(m[...], wr[own, :])
    recv_rest[...] = wr[other, :]


def other_features_kernel(part, rest, other, *outs):
    width = outs[0].shape[1]
    for c, out in enumerate(outs):
        lanes = slice(c * width, (c + 1) * width)
        out[...] = (part[:, lanes] + dot(other[...], rest[:, lanes])).astype(BF16)


def project(grid, mesh, w_send, w_recv, n_chunks):
    grid_other, mesh_other = swap(grid), swap(mesh)
    hidden, feats = w_send.shape[1], grid.shape[1]
    parts = call(
        own_features_kernel,
        [
            shape_of((grid.shape[0], hidden), F32),
            shape_of((mesh.shape[0], hidden), F32),
            shape_of((feats, hidden), BF16),
            shape_of((feats, hidden), BF16),
        ],
        position("feat"),
        *[pltpu.with_memory_space_constraint(x, pltpu.HBM) for x in (grid, mesh, w_send, w_recv)],
        specs=[SMEM] + [HBM] * 4,
        scratch=[pltpu.VMEM(x.shape, BF16) for x in (w_send, grid, w_recv, mesh)] + [pltpu.SemaphoreType.DMA((16,))],
        name="own_features",
        mib=16,
    )
    grid_part, mesh_part, send_rest, recv_rest = parts
    chunk = shape_of((grid.shape[0], hidden // n_chunks), BF16)
    chunks = call(
        other_features_kernel, [chunk] * n_chunks, grid_part, send_rest, grid_other, name="other_grid_features"
    )
    chunks, mesh_part = lax.optimization_barrier((chunks, mesh_part))
    (mesh_proj,) = call(
        other_features_kernel,
        [shape_of((mesh.shape[0], hidden), BF16)],
        mesh_part,
        recv_rest,
        mesh_other,
        name="other_mesh_features",
    )
    return chunks, mesh_proj, mesh_other


def across(row):
    return jnp.transpose(jnp.broadcast_to(row.astype(F32), (LANES, LANES))).astype(I32)


def slots_of(ref, n, cap):
    return ref[:, pl.ds(pl.multiple_of(n * cap, cap), cap)]


def one_hot_rows(row, width, at):
    return (across(row[:, at : at + LANES])[:, :1] == iota((LANES, width), 1)).astype(BF16)


def pack_own_kernel(bits, me, send, g0, g1, *outs):
    width, cap = g0.shape[1], outs[0].shape[0]
    for k, out in zip(bits, outs):
        ids = slots_of(send, me[0] ^ k, cap)
        for at in range(0, cap, LANES):
            hot = one_hot_rows(ids, g0.shape[0], at)
            out[at : at + LANES, :width] = dot(hot, g0[...]).astype(BF16)
            out[at : at + LANES, width:] = dot(hot, g1[...]).astype(BF16)


def prepare_kernel(half, me, send_mirror, recv, mesh_proj, bias, pick, into, term):
    cap = pick.shape[0] // half
    for k in range(half):
        ids, rows = slots_of(send_mirror, me[0] ^ k, cap), slots_of(recv, me[0] ^ k ^ half, cap)
        first = k * cap
        into[:, first : first + cap] = (iota((into.shape[0], cap), 0) == rows).astype(BF16)
        for at in range(0, cap, LANES):
            here = slice(first + at, first + at + LANES)
            pick[here, :] = one_hot_rows(ids, pick.shape[1], at)
            term[here, :] = dot(one_hot_rows(rows, mesh_proj.shape[0], at), mesh_proj[...]) + bias[...]


def add_slots(total, grid, rows, mesh_proj, bias):
    hot = [one_hot_rows(rows, mesh_proj.shape[0], at) for at in range(0, rows.shape[1], LANES)]
    term = dot(jnp.concatenate(hot, axis=0), mesh_proj[...])
    into = (iota((mesh_proj.shape[0], rows.shape[1]), 0) == rows).astype(BF16)
    return total + dot(into, silu_bf16(grid + term + bias[...]))


def local_sums_kernel(cap, me, send, recv, g0, g1, mesh_proj, bias, out):
    ids, rows = slots_of(send, me[0], cap), slots_of(recv, me[0], cap)
    hot = jnp.concatenate([one_hot_rows(ids, g0.shape[0], at) for at in range(0, cap, LANES)], axis=0)
    grid = jnp.concatenate([dot(hot, g0[...]), dot(hot, g1[...])], axis=1)
    out[...] = add_slots(0.0, grid, rows, mesh_proj, bias)


def arrived_sums_kernel(cap, me, recv, mesh_proj, bias, start, *refs):
    *blocks, out = refs
    total = start[...]
    for k, block in enumerate(blocks, 1):
        total = add_slots(total, block[...].astype(F32), slots_of(recv, me[0] ^ k, cap), mesh_proj, bias)
    out[...] = total


def pack_mirror_kernel(pick, mirrored, *outs):
    cap = outs[0].shape[0]
    for k, out in enumerate(outs, 1):
        out[...] = dot(pick[k * cap : (k + 1) * cap, :], mirrored[...]).astype(BF16)


def mirror_sums_kernel(chunk, first, pick, mirrored, into, term, total, *refs):
    *blocks, out = refs
    width = out.shape[1]
    lanes = slice(chunk * width, (chunk + 1) * width)
    cap = into.shape[1] // 4
    if first:
        blocks = [dot(pick[:cap, :], mirrored[...])]
        sums = total[:, lanes]
    else:
        sums = total[...]
    for k, block in enumerate(blocks, 0 if first else 1):
        rows = slice(k * cap, (k + 1) * cap)
        hidden = silu_bf16(block[...].astype(F32) + term[rows, lanes])
        sums += dot(into[:, rows], hidden)
    out[...] = sums.astype(out.dtype)


def sums_by_halves(grid_chunks, mesh_rproj, bias, send_grid, recv_row, n_dom, select, lists):
    half = n_dom // 2
    mesh_rows, hidden = mesh_rproj.shape
    grid_rows, width = grid_chunks[0].shape
    cap = send_grid.shape[1] // n_dom
    me, bias = position("dom"), bias[None, :]

    def pack_own(*bits):
        blocks = call(
            functools.partial(pack_own_kernel, bits),
            [shape_of((cap, hidden), BF16)] * len(bits),
            me,
            send_grid,
            *grid_chunks,
            specs=[SMEM] + [VMEM] * 3,
            name="pack_own",
        )
        return blocks

    packed = pack_own(3, 2)
    packed, first = lax.optimization_barrier((packed, grid_chunks[0]))
    arrived = {k: from_xor(block, k, n_dom) for k, block in zip((3, 2), packed)}
    mirrored = [from_xor(first, half, n_dom)]
    send_mirror = from_xor(send_grid, half, n_dom)
    own = call(
        functools.partial(local_sums_kernel, cap),
        shape_of((mesh_rows, hidden), F32),
        me,
        send_grid,
        recv_row,
        *grid_chunks,
        mesh_rproj,
        bias,
        specs=[SMEM] + [VMEM] * 6,
        name="local_sums",
    )
    own, packed, lists = lax.optimization_barrier((own, pack_own(1), lists))
    arrived[1] = from_xor(packed[0], 1, n_dom)
    selections = select(me, *lists)
    send_mirror, later, selections = lax.optimization_barrier((send_mirror, grid_chunks[1], selections))
    mirrored.append(from_xor(later, half, n_dom))
    arrived = [arrived[k] for k in range(1, half)]
    pick, into, term = call(
        functools.partial(prepare_kernel, half),
        [
            shape_of((half * cap, grid_rows), BF16),
            shape_of((mesh_rows, half * cap), BF16),
            shape_of((half * cap, hidden), F32),
        ],
        me,
        send_mirror,
        recv_row,
        mesh_rproj,
        bias,
        specs=[SMEM] + [VMEM] * 4,
        name="prepare",
    )
    arrived, mirrored[1] = lax.optimization_barrier((arrived, mirrored[1]))
    own = call(
        functools.partial(arrived_sums_kernel, cap),
        shape_of((mesh_rows, hidden), F32),
        me,
        recv_row,
        mesh_rproj,
        bias,
        own,
        *arrived,
        specs=[SMEM] + [VMEM] * (4 + len(arrived)),
        name="arrived_sums",
    )
    chunks = []
    for c in range(2):
        blocks = call(
            pack_mirror_kernel, [shape_of((cap, width), BF16)] * (half - 1), pick, mirrored[c], name="pack_mirror"
        )
        blocks = [from_xor(block, k, n_dom) for k, block in enumerate(blocks, 1)]
        total = call(
            functools.partial(mirror_sums_kernel, c, True),
            shape_of((mesh_rows, width), F32),
            pick,
            mirrored[c],
            into,
            term,
            own,
            name="own_mirror_sums",
        )
        chunks.append(
            call(
                functools.partial(mirror_sums_kernel, c, False),
                shape_of((mesh_rows, width), BF16),
                pick,
                mirrored[c],
                into,
                term,
                total,
                *blocks,
                name="mirror_sums",
            )
        )
    return chunks, selections


def sums_by_all_to_all(grid_chunks, mesh_rproj, bias, send_grid, recv_row, n_dom, select, lists):
    def rows_of(table, index):
        hot = index[0][:, None] == iota((index.shape[1], table.shape[0]), 1)
        return dot(hot.astype(BF16), table)

    packed = rows_of(grid_chunks[0], send_grid).astype(BF16)
    arrived = lax.all_to_all(packed, "dom", split_axis=0, concat_axis=0, tiled=True)
    hidden = silu_bf16(arrived.astype(F32) + rows_of(mesh_rproj, recv_row) + bias[None, :])
    into = iota((mesh_rproj.shape[0], recv_row.shape[1]), 0) == recv_row
    return [dot(into.astype(BF16), hidden).astype(BF16)], select(position("dom"), *lists)


def list_rows(ref, me, k, blocks):
    size = ref.shape[1] // blocks
    return slots_of(ref, me ^ k, size) if blocks > 1 else ref[...]


def select_kernel(blocks, me, halo_rows, src, dst, halo_pick, near_src, near_dst, far_src, into):
    mesh_rows = into.shape[0]
    size = halo_pick.shape[0] // blocks
    for k in range(blocks):
        rows = list_rows(halo_rows, me[0], k, blocks)
        for a in range(0, size, LANES):
            halo_pick[k * size + a : k * size + a + LANES, :] = one_hot_rows(rows, mesh_rows, a)
    for b in range(src.shape[0]):
        rows = slice(b * LANES, (b + 1) * LANES)
        senders, receivers = src[b : b + 1, :], dst[b : b + 1, :]
        far = senders - mesh_rows
        if blocks > 1:
            far = jnp.where(far < 0, far, ((far // size) ^ me[0]) * size + far % size)
        near_src[rows, :] = one_hot_rows(senders, mesh_rows, 0)
        near_dst[rows, :] = one_hot_rows(receivers, mesh_rows, 0)
        far_src[rows, :] = one_hot_rows(far, far_src.shape[1], 0)
        into[:, rows] = (iota((mesh_rows, LANES), 0) == receivers).astype(BF16)


def encode_base_kernel(n_chunks, feat, *refs):
    chunks, others = refs[:n_chunks], refs[n_chunks : 2 * n_chunks]
    mesh_own, mesh_other, w_own, w_other, w2_own, w2_other, base, w2 = refs[2 * n_chunks :]
    feats = mesh_own.shape[1]
    own, rest = halves_of(feat[0], feats)
    base[:, own] = mesh_own[...].astype(F32)
    base[:, rest] = mesh_other[...].astype(F32)
    at = 0
    for mine, other in zip(chunks, others):
        rows = slice(at, at + mine.shape[1])
        base[...] += dot(mine[...], w_own[rows, :]) + dot(other[...], w_other[rows, :])
        at += mine.shape[1]
    w2[: w2_own.shape[0], :] = w2_own[:, own]
    w2[w2_own.shape[0] :, :] = w2_other[:, own]


def encode_kernel(first, base, mine, other, w_own, w_other, w_send, pick, full, send_proj, *halo):
    rows = slice(first, first + mine.shape[1])
    full[...] = (base[...] + dot(mine[...], w_own[rows, :]) + dot(other[...], w_other[rows, :])).astype(BF16)
    send_proj[...] = dot(full[...], w_send[...]).astype(BF16)
    size = halo[0].shape[0]
    for k, out in enumerate(halo):
        out[...] = dot(pick[k * size : (k + 1) * size, :], send_proj[...]).astype(BF16)


def near_edges_kernel(feat, full, send_proj, w_recv, bias, near_src, near_dst, near, encoded):
    own, _ = halves_of(feat[0], encoded.shape[1])
    encoded[...] = full[:, own]
    recv_proj = dot(full[...], w_recv[...]).astype(BF16)
    for at in range(0, near.shape[0], STEP):
        rows = slice(at, at + STEP)
        near[rows, :] = dot(near_src[rows, :], send_proj[...]) + dot(near_dst[rows, :], recv_proj) + bias[...]


def edge_sums_kernel(near, far_pick, into, *refs):
    *halo, out, table = refs
    size = halo[0].shape[0]
    for k, block in enumerate(halo):
        table[k * size : (k + 1) * size, :] = block[...]
    total = jnp.zeros(out.shape, F32)
    for at in range(0, near.shape[0], STEP):
        rows = slice(at, at + STEP)
        hidden = silu_bf16(near[rows, :] + dot(far_pick[rows, :], table[...]))
        total += dot(into[:, rows], hidden)
    out[...] = total.astype(BF16)


def own_output_kernel(encoded, mine, w_out, out):
    out[...] = encoded[...].astype(F32) + dot(mine[...], w_out[: mine.shape[1], :])


def output_kernel(part, other, w_out, out):
    out[...] = (part[...] + dot(other[...], w_out[other.shape[1] :, :])).astype(BF16)


def shards(
    grid_lat,
    mesh_lat,
    w_grid_send,
    w_grid_recv,
    g2m_bias,
    w_grid_out,
    w_edge_send,
    w_edge_recv,
    edge_bias,
    w_edge_out,
    send_grid,
    recv_row,
    halo_rows,
    edge_src,
    edge_dst,
):
    n_dom = lax.axis_size("dom")
    mesh_rows, feats = mesh_lat.shape
    hidden = w_grid_send.shape[1]
    halves = n_dom == 8
    grid_chunks, mesh_rproj, mesh_other = project(grid_lat, mesh_lat, w_grid_send, w_grid_recv, 2 if halves else 1)
    grid_chunks, mesh_rproj, send_grid, recv_row, w_other, w2_other = lax.optimization_barrier(
        (grid_chunks, mesh_rproj, send_grid, recv_row, swap(w_grid_out), swap(w_edge_out))
    )
    me, feat = position("dom"), position("feat")
    blocks = n_dom if halves else 1
    n_halo, edges = halo_rows.shape[1], edge_src.shape[0] * edge_src.shape[1]
    def select(me, halo_rows, src, dst):
        return call(
            functools.partial(select_kernel, blocks),
            [
                shape_of((n_halo, mesh_rows), BF16),
                shape_of((edges, mesh_rows), BF16),
                shape_of((edges, mesh_rows), BF16),
                shape_of((edges, n_halo), BF16),
                shape_of((mesh_rows, edges), BF16),
            ],
            me,
            halo_rows,
            src,
            dst,
            specs=[SMEM] + [VMEM] * 3,
            name="select",
        )

    sums = sums_by_halves if halves else sums_by_all_to_all
    lists = (halo_rows, edge_src, edge_dst)
    chunks, selections = sums(grid_chunks, mesh_rproj, g2m_bias, send_grid, recv_row, n_dom, select, lists)
    pick, near_src, near_dst, far_src, into = selections
    *early, last = chunks
    base, w_out = call(
        functools.partial(encode_base_kernel, len(early)),
        [shape_of((mesh_rows, 2 * feats), F32), shape_of((2 * w_edge_out.shape[0], feats), BF16)],
        feat,
        *early,
        *[swap(chunk) for chunk in early],
        mesh_lat,
        mesh_other,
        w_grid_out,
        w_other,
        w_edge_out,
        w2_other,
        specs=[SMEM] + [VMEM] * (2 * len(early) + 6),
        name="encode_base",
    )
    full, send_proj, *halo = call(
        functools.partial(encode_kernel, hidden - last.shape[1]),
        [shape_of((mesh_rows, 2 * feats), BF16), shape_of((mesh_rows, hidden), BF16)]
        + [shape_of((n_halo // blocks, hidden), BF16)] * blocks,
        base,
        last,
        swap(last),
        w_grid_out,
        w_other,
        w_edge_send,
        pick,
        name="encode",
    )
    if halves:
        arrived = {k: from_xor(halo[k], k, n_dom) for k in (6, 7, 4, 5, 3, 2, 1)}
        halo = [halo[0]] + [arrived[k] for k in range(1, n_dom)]
    else:
        halo = [lax.all_to_all(halo[0], "dom", split_axis=0, concat_axis=0, tiled=True)]
    near, mesh_encoded = call(
        near_edges_kernel,
        [shape_of((edges, hidden), F32), shape_of((mesh_rows, feats), BF16)],
        feat,
        full,
        send_proj,
        w_edge_recv,
        edge_bias[None, :],
        near_src,
        near_dst,
        specs=[SMEM] + [VMEM] * 6,
        name="near_edges",
    )
    proc_sum = call(
        edge_sums_kernel,
        shape_of((mesh_rows, hidden), BF16),
        near,
        far_src,
        into,
        *halo,
        scratch=[pltpu.VMEM((n_halo, hidden), BF16)],
        name="edge_sums",
    )
    part = call(
        own_output_kernel, shape_of((mesh_rows, feats), F32), mesh_encoded, proc_sum, w_out, name="own_output"
    )
    mesh_out = call(
        output_kernel, shape_of((mesh_rows, feats), BF16), part, swap(proc_sum), w_out, name="output"
    )
    return (mesh_encoded, mesh_out)


def solution(mesh):
    rows = P(("member", "dom"), "feat")
    columns, lists = P(None, "feat"), P("dom", None)
    placed = (rows, rows, columns, columns, P("feat"), P("feat", None), columns, columns, P("feat"), P("feat", None))
    return jax.shard_map(
        shards,
        mesh=mesh,
        in_specs=placed + (lists,) * 5,
        out_specs=(rows, rows),
        check_vma=False,
    )
```

```python
import functools

import jax
import jax.numpy as jnp
from jax import lax
from jax.experimental import pallas as pl
from jax.experimental.pallas import tpu as pltpu
from jax.sharding import PartitionSpec as P

BF16, F32, I32 = jnp.bfloat16, jnp.float32, jnp.int32
LANES = 128
STEP = 256
DIGIT = 64
MIB = 24
SMEM = pl.BlockSpec(memory_space=pltpu.SMEM)
VMEM = pl.BlockSpec(memory_space=pltpu.VMEM)
HBM = pl.BlockSpec(memory_space=pltpu.HBM)


def dot(a, b):
    return jnp.dot(a, b, preferred_element_type=F32)


def iota(shape, axis):
    return lax.broadcasted_iota(I32, shape, axis)


def silu_bf16(v):
    return (v / (1.0 + jnp.exp(-v))).astype(BF16)


def shape_of(shape, dtype):
    return jax.ShapeDtypeStruct(shape, dtype)


def position(axis):
    return lax.axis_index(axis).astype(I32).reshape(1)


def swap(x):
    return lax.ppermute(x, "feat", [(0, 1), (1, 0)])


def from_xor(x, bits, n_dom):
    return lax.ppermute(x, "dom", [(i, i ^ bits) for i in range(n_dom)])


def call(kernel, out_shape, *args, specs=None, outs=None, name, scratch=(), mib=MIB):
    return pl.pallas_call(
        kernel,
        out_shape=out_shape,
        in_specs=[VMEM] * len(args) if specs is None else specs,
        out_specs=jax.tree.map(lambda _: VMEM, out_shape) if outs is None else outs,
        scratch_shapes=scratch,
        compiler_params=pltpu.CompilerParams(vmem_limit_bytes=mib << 20),
        name=name,
    )(*args)


def halves_of(feat, size):
    own = pl.ds(pl.multiple_of(feat * size, size), size)
    other = pl.ds(pl.multiple_of((1 - feat) * size, size), size)
    return own, other


def start_copies(source, target, sems, first, pieces):
    rows = source.shape[0] // pieces
    copies = []
    for n in range(pieces):
        part = pl.ds(n * rows, rows)
        copies.append(pltpu.make_async_copy(source.at[part], target.at[part], sems.at[first + n]))
        copies[-1].start()
    return copies


def wait_copies(copies):
    for copy in copies:
        copy.wait()


def own_features_kernel(feat, grid, mesh, w_send, w_recv, send, grid_part, mesh_part, send_rest, recv_rest, list_out, *scratch):
    ws, g, wr, m, ids, sems = scratch
    first = start_copies(w_send, ws, sems, 0, 4) + start_copies(grid, g, sems, 4, 4)
    second = start_copies(w_recv, wr, sems, 8, 4) + start_copies(mesh, m, sems, 12, 4)
    second += start_copies(send, ids, sems, 16, 1)
    own, other = halves_of(feat[0], g.shape[1])
    wait_copies(first)
    grid_part[...] = dot(g[...], ws[own, :])
    send_rest[...] = ws[other, :]
    wait_copies(second)
    mesh_part[...] = dot(m[...], wr[own, :])
    recv_rest[...] = wr[other, :]
    rows = jnp.concatenate([ids[:, a : a + LANES] for a in range(0, ids.shape[1], LANES)], axis=0)
    list_out[...] = jnp.concatenate([rows // DIGIT, rows % DIGIT], axis=0).astype(F32).astype(BF16)


def other_features_kernel(part, rest, other, *outs):
    width = outs[0].shape[1]
    for c, out in enumerate(outs):
        lanes = slice(c * width, (c + 1) * width)
        out[...] = (part[:, lanes] + dot(other[...], rest[:, lanes])).astype(BF16)


def with_list_kernel(part, rest, other, digits, *outs):
    *chunks, first = outs
    other_features_kernel(part, rest, other, *chunks)
    first[: part.shape[0], :] = chunks[0][...]
    first[part.shape[0] :, :] = digits[...]


def project(grid, mesh, w_send, w_recv, send, n_chunks):
    grid_other, mesh_other = swap(grid), swap(mesh)
    hidden, feats = w_send.shape[1], grid.shape[1]
    parts = call(
        own_features_kernel,
        [
            shape_of((grid.shape[0], hidden), F32),
            shape_of((mesh.shape[0], hidden), F32),
            shape_of((feats, hidden), BF16),
            shape_of((feats, hidden), BF16),
            shape_of((2 * send.shape[1] // LANES, LANES), BF16),
        ],
        position("feat"),
        *[pltpu.with_memory_space_constraint(x, pltpu.HBM) for x in (grid, mesh, w_send, w_recv, send)],
        specs=[SMEM] + [HBM] * 5,
        scratch=[pltpu.VMEM(x.shape, x.dtype) for x in (w_send, grid, w_recv, mesh, send)]
        + [pltpu.SemaphoreType.DMA((17,))],
        name="own_features",
        mib=16,
    )
    grid_part, mesh_part, send_rest, recv_rest, digits = parts
    chunk = shape_of((grid.shape[0], hidden // n_chunks), BF16)
    if n_chunks > 1:
        first = shape_of((grid.shape[0] + digits.shape[0], chunk.shape[1]), BF16)
        chunks = call(
            with_list_kernel,
            [chunk] * n_chunks + [first],
            grid_part,
            send_rest,
            grid_other,
            digits,
            name="other_grid_features",
        )
    else:
        chunks = call(other_features_kernel, [chunk], grid_part, send_rest, grid_other, name="other_grid_features")
    chunks, mesh_part = lax.optimization_barrier((chunks, mesh_part))
    (mesh_proj,) = call(
        other_features_kernel,
        [shape_of((mesh.shape[0], hidden), BF16)],
        mesh_part,
        recv_rest,
        mesh_other,
        name="other_mesh_features",
    )
    return chunks, mesh_proj, mesh_other


def across(row):
    return jnp.transpose(jnp.broadcast_to(row.astype(F32), (LANES, LANES))).astype(I32)


def slots_of(ref, n, cap):
    return ref[:, pl.ds(pl.multiple_of(n * cap, cap), cap)]


def one_hot_rows(row, width, at):
    return (across(row[:, at : at + LANES])[:, :1] == iota((LANES, width), 1)).astype(BF16)


def pack_own_kernel(bits, me, send, g0, g1, *outs):
    width, cap = g0.shape[1], outs[0].shape[0]
    for k, out in zip(bits, outs):
        ids = slots_of(send, me[0] ^ k, cap)
        for at in range(0, cap, LANES):
            hot = one_hot_rows(ids, g0.shape[0], at)
            out[at : at + LANES, :width] = dot(hot, g0[...]).astype(BF16)
            out[at : at + LANES, width:] = dot(hot, g1[...]).astype(BF16)


def prepare_kernel(half, me, recv, mesh_proj, bias, into, term):
    cap = term.shape[0] // half
    for k in range(half):
        rows = slots_of(recv, me[0] ^ k ^ half, cap)
        first = k * cap
        into[:, first : first + cap] = (iota((into.shape[0], cap), 0) == rows).astype(BF16)
        for at in range(0, cap, LANES):
            here = slice(first + at, first + at + LANES)
            term[here, :] = dot(one_hot_rows(rows, mesh_proj.shape[0], at), mesh_proj[...]) + bias[...]


def aside_kernel(half, cap, blocks, me, send, recv, g0, g1, mesh_proj, bias, halo_rows, src, dst, *outs):
    packed, sums, into, term, *selections = outs
    pack_own_kernel((1,), me, send, g0, g1, packed)
    local_sums_kernel(cap, me, send, recv, g0, g1, mesh_proj, bias, sums)
    prepare_kernel(half, me, recv, mesh_proj, bias, into, term)
    select_kernel(blocks, me, halo_rows, src, dst, *selections)


def pick_kernel(half, me, mirrored, pick, ids):
    cap, grid_rows = pick.shape[0] // half, pick.shape[1]
    lines = ids.shape[0]
    digits = mirrored[grid_rows:, :].astype(F32).astype(I32)
    ids[...] = digits[:lines, :] * DIGIT + digits[lines:, :]
    for k in range(half):
        for n in range(cap // LANES):
            row = ids[pl.ds((me[0] ^ k) * (cap // LANES) + n, 1), :]
            first = k * cap + n * LANES
            pick[first : first + LANES, :] = one_hot_rows(row, grid_rows, 0)


def add_slots(total, grid, rows, mesh_proj, bias):
    hot = [one_hot_rows(rows, mesh_proj.shape[0], at) for at in range(0, rows.shape[1], LANES)]
    term = dot(jnp.concatenate(hot, axis=0), mesh_proj[...])
    into = (iota((mesh_proj.shape[0], rows.shape[1]), 0) == rows).astype(BF16)
    return total + dot(into, silu_bf16(grid + term + bias[...]))


def local_sums_kernel(cap, me, send, recv, g0, g1, mesh_proj, bias, out):
    ids, rows = slots_of(send, me[0], cap), slots_of(recv, me[0], cap)
    hot = jnp.concatenate([one_hot_rows(ids, g0.shape[0], at) for at in range(0, cap, LANES)], axis=0)
    grid = jnp.concatenate([dot(hot, g0[...]), dot(hot, g1[...])], axis=1)
    out[...] = add_slots(0.0, grid, rows, mesh_proj, bias)


def arrived_sums_kernel(cap, me, recv, mesh_proj, bias, start, *refs):
    *blocks, out = refs
    blocks.reverse()
    total = start[...]
    for k, block in enumerate(blocks, 1):
        total = add_slots(total, block[...].astype(F32), slots_of(recv, me[0] ^ k, cap), mesh_proj, bias)
    out[...] = total


def pack_mirror_kernel(pick, mirrored, *outs):
    cap = outs[0].shape[0]
    for k, out in enumerate(outs, 1):
        out[...] = dot(pick[k * cap : (k + 1) * cap, :], mirrored[: pick.shape[1], :]).astype(BF16)


def mirror_sums_kernel(chunk, first, pick, mirrored, into, term, total, *refs):
    *blocks, out = refs
    width = out.shape[1]
    lanes = slice(chunk * width, (chunk + 1) * width)
    cap = into.shape[1] // 4
    if first:
        blocks = [dot(pick[:cap, :], mirrored[: pick.shape[1], :])]
        sums = total[:, lanes]
    else:
        blocks.reverse()
        sums = total[...]
    for k, block in enumerate(blocks, 0 if first else 1):
        rows = slice(k * cap, (k + 1) * cap)
        hidden = silu_bf16(block[...].astype(F32) + term[rows, lanes])
        sums += dot(into[:, rows], hidden)
    out[...] = sums.astype(out.dtype)


def sums_by_halves(grid_chunks, mesh_rproj, bias, send_grid, recv_row, n_dom, select, lists):
    half = n_dom // 2
    mesh_rows, hidden = mesh_rproj.shape
    *grid_chunks, with_list = grid_chunks
    grid_rows, width = grid_chunks[0].shape
    cap = send_grid.shape[1] // n_dom
    me, bias = position("dom"), bias[None, :]

    def pack_own(*bits):
        blocks = call(
            functools.partial(pack_own_kernel, bits),
            [shape_of((cap, hidden), BF16)] * len(bits),
            me,
            send_grid,
            *grid_chunks,
            specs=[SMEM] + [VMEM] * 3,
            name="pack_own",
        )
        return blocks

    packed = pack_own(3, 2)
    packed, with_list, grid_chunks = lax.optimization_barrier((packed, with_list, grid_chunks))
    arrived = {k: from_xor(block, k, n_dom) for k, block in zip((3, 2), packed)}
    mirrored = [from_xor(with_list, half, n_dom)]
    selection_shapes, blocks = select
    packed, own, into, term, *selections = call(
        functools.partial(aside_kernel, half, cap, blocks),
        [
            shape_of((cap, hidden), BF16),
            shape_of((mesh_rows, hidden), F32),
            shape_of((mesh_rows, half * cap), BF16),
            shape_of((half * cap, hidden), F32),
            *selection_shapes,
        ],
        me,
        send_grid,
        recv_row,
        *grid_chunks,
        mesh_rproj,
        bias,
        *lists,
        specs=[SMEM] + [VMEM] * (6 + len(lists)),
        name="aside",
    )
    arrived[1] = from_xor(packed, 1, n_dom)
    arrived = [arrived[k] for k in range(1, half)]
    mirrored.append(from_xor(grid_chunks[1], half, n_dom))
    own, into, term, selections, mirrored[0] = lax.optimization_barrier((own, into, term, selections, mirrored[0]))
    pick = call(
        functools.partial(pick_kernel, half),
        shape_of((half * cap, grid_rows), BF16),
        me,
        mirrored[0],
        specs=[SMEM, VMEM],
        scratch=[pltpu.VMEM((send_grid.shape[1] // LANES, LANES), I32)],
        name="pick",
    )
    own = call(
        functools.partial(arrived_sums_kernel, cap),
        shape_of((mesh_rows, hidden), F32),
        me,
        recv_row,
        mesh_rproj,
        bias,
        own,
        *arrived[::-1],
        specs=[SMEM] + [VMEM] * (4 + len(arrived)),
        name="arrived_sums",
    )
    chunks = []
    for c in range(2):
        blocks = call(
            pack_mirror_kernel, [shape_of((cap, width), BF16)] * (half - 1), pick, mirrored[c], name="pack_mirror"
        )
        blocks = [from_xor(block, k, n_dom) for k, block in enumerate(blocks, 1)]
        total = call(
            functools.partial(mirror_sums_kernel, c, True),
            shape_of((mesh_rows, width), F32),
            pick,
            mirrored[c],
            into,
            term,
            own,
            name="own_mirror_sums",
        )
        chunks.append(
            call(
                functools.partial(mirror_sums_kernel, c, False),
                shape_of((mesh_rows, width), BF16),
                pick,
                mirrored[c],
                into,
                term,
                total,
                *blocks[::-1],
                name="mirror_sums",
            )
        )
    return chunks, selections


def sums_by_all_to_all(grid_chunks, mesh_rproj, bias, send_grid, recv_row, n_dom, select, lists):
    def rows_of(table, index):
        hot = index[0][:, None] == iota((index.shape[1], table.shape[0]), 1)
        return dot(hot.astype(BF16), table)

    packed = rows_of(grid_chunks[0], send_grid).astype(BF16)
    arrived = lax.all_to_all(packed, "dom", split_axis=0, concat_axis=0, tiled=True)
    hidden = silu_bf16(arrived.astype(F32) + rows_of(mesh_rproj, recv_row) + bias[None, :])
    into = iota((mesh_rproj.shape[0], recv_row.shape[1]), 0) == recv_row
    selection_shapes, blocks = select
    selections = call(
        functools.partial(select_kernel, blocks),
        selection_shapes,
        position("dom"),
        *lists,
        specs=[SMEM] + [VMEM] * len(lists),
        name="select",
    )
    return [dot(into.astype(BF16), hidden).astype(BF16)], selections


def list_rows(ref, me, k, blocks):
    size = ref.shape[1] // blocks
    return slots_of(ref, me ^ k, size) if blocks > 1 else ref[...]


def select_kernel(blocks, me, halo_rows, src, dst, halo_pick, near_src, near_dst, far_src, into):
    mesh_rows = into.shape[0]
    size = halo_pick.shape[0] // blocks
    for k in range(blocks):
        rows = list_rows(halo_rows, me[0], k, blocks)
        for a in range(0, size, LANES):
            halo_pick[k * size + a : k * size + a + LANES, :] = one_hot_rows(rows, mesh_rows, a)
    for b in range(src.shape[0]):
        rows = slice(b * LANES, (b + 1) * LANES)
        senders, receivers = src[b : b + 1, :], dst[b : b + 1, :]
        far = senders - mesh_rows
        if blocks > 1:
            far = jnp.where(far < 0, far, ((far // size) ^ me[0]) * size + far % size)
        near_src[rows, :] = one_hot_rows(senders, mesh_rows, 0)
        near_dst[rows, :] = one_hot_rows(receivers, mesh_rows, 0)
        far_src[rows, :] = one_hot_rows(far, far_src.shape[1], 0)
        into[:, rows] = (iota((mesh_rows, LANES), 0) == receivers).astype(BF16)


def encode_base_kernel(n_chunks, feat, *refs):
    chunks, others = refs[:n_chunks], refs[n_chunks : 2 * n_chunks]
    mesh_own, mesh_other, w_own, w_other, w2_own, w2_other, base, w2 = refs[2 * n_chunks :]
    feats = mesh_own.shape[1]
    own, rest = halves_of(feat[0], feats)
    base[:, own] = mesh_own[...].astype(F32)
    base[:, rest] = mesh_other[...].astype(F32)
    at = 0
    for mine, other in zip(chunks, others):
        rows = slice(at, at + mine.shape[1])
        base[...] += dot(mine[...], w_own[rows, :]) + dot(other[...], w_other[rows, :])
        at += mine.shape[1]
    w2[: w2_own.shape[0], :] = w2_own[:, own]
    w2[w2_own.shape[0] :, :] = w2_other[:, own]


def encode_kernel(first, base, mine, other, w_own, w_other, w_send, pick, full, send_proj, *halo):
    rows = slice(first, first + mine.shape[1])
    full[...] = (base[...] + dot(mine[...], w_own[rows, :]) + dot(other[...], w_other[rows, :])).astype(BF16)
    send_proj[...] = dot(full[...], w_send[...]).astype(BF16)
    size = halo[0].shape[0]
    for k, out in enumerate(halo):
        out[...] = dot(pick[k * size : (k + 1) * size, :], send_proj[...]).astype(BF16)


def near_edges_kernel(feat, full, send_proj, w_recv, bias, near_src, near_dst, near, encoded):
    own, _ = halves_of(feat[0], encoded.shape[1])
    encoded[...] = full[:, own]
    recv_proj = dot(full[...], w_recv[...]).astype(BF16)
    for at in range(0, near.shape[0], STEP):
        rows = slice(at, at + STEP)
        near[rows, :] = dot(near_src[rows, :], send_proj[...]) + dot(near_dst[rows, :], recv_proj) + bias[...]


def edge_sums_kernel(near, far_pick, into, *refs):
    *halo, out, table = refs
    halo.reverse()
    size = halo[0].shape[0]
    for k, block in enumerate(halo):
        table[k * size : (k + 1) * size, :] = block[...]
    total = jnp.zeros(out.shape, F32)
    for at in range(0, near.shape[0], STEP):
        rows = slice(at, at + STEP)
        hidden = silu_bf16(near[rows, :] + dot(far_pick[rows, :], table[...]))
        total += dot(into[:, rows], hidden)
    out[...] = total.astype(BF16)


def own_output_kernel(encoded, mine, w_out, out):
    out[...] = encoded[...].astype(F32) + dot(mine[...], w_out[: mine.shape[1], :])


def output_kernel(part, other, w_out, out):
    out[...] = (part[...] + dot(other[...], w_out[other.shape[1] :, :])).astype(BF16)


def shards(
    grid_lat,
    mesh_lat,
    w_grid_send,
    w_grid_recv,
    g2m_bias,
    w_grid_out,
    w_edge_send,
    w_edge_recv,
    edge_bias,
    w_edge_out,
    send_grid,
    recv_row,
    halo_rows,
    edge_src,
    edge_dst,
):
    n_dom = lax.axis_size("dom")
    mesh_rows, feats = mesh_lat.shape
    hidden = w_grid_send.shape[1]
    halves = n_dom == 8
    grid_chunks, mesh_rproj, mesh_other = project(
        grid_lat, mesh_lat, w_grid_send, w_grid_recv, send_grid, 2 if halves else 1
    )
    grid_chunks, mesh_rproj, send_grid, recv_row, w_other, w2_other = lax.optimization_barrier(
        (grid_chunks, mesh_rproj, send_grid, recv_row, swap(w_grid_out), swap(w_edge_out))
    )
    me, feat = position("dom"), position("feat")
    blocks = n_dom if halves else 1
    n_halo, edges = halo_rows.shape[1], edge_src.shape[0] * edge_src.shape[1]
    select = (
        [
            shape_of((n_halo, mesh_rows), BF16),
            shape_of((edges, mesh_rows), BF16),
            shape_of((edges, mesh_rows), BF16),
            shape_of((edges, n_halo), BF16),
            shape_of((mesh_rows, edges), BF16),
        ],
        blocks,
    )
    sums = sums_by_halves if halves else sums_by_all_to_all
    lists = (halo_rows, edge_src, edge_dst)
    chunks, selections = sums(grid_chunks, mesh_rproj, g2m_bias, send_grid, recv_row, n_dom, select, lists)
    pick, near_src, near_dst, far_src, into = selections
    *early, last = chunks
    base, w_out = call(
        functools.partial(encode_base_kernel, len(early)),
        [shape_of((mesh_rows, 2 * feats), F32), shape_of((2 * w_edge_out.shape[0], feats), BF16)],
        feat,
        *early,
        *[swap(chunk) for chunk in early],
        mesh_lat,
        mesh_other,
        w_grid_out,
        w_other,
        w_edge_out,
        w2_other,
        specs=[SMEM] + [VMEM] * (2 * len(early) + 6),
        name="encode_base",
    )
    full, send_proj, *halo = call(
        functools.partial(encode_kernel, hidden - last.shape[1]),
        [shape_of((mesh_rows, 2 * feats), BF16), shape_of((mesh_rows, hidden), BF16)]
        + [shape_of((n_halo // blocks, hidden), BF16)] * blocks,
        base,
        last,
        swap(last),
        w_grid_out,
        w_other,
        w_edge_send,
        pick,
        name="encode",
    )
    if halves:
        arrived = {k: from_xor(halo[k], k, n_dom) for k in (6, 7, 4, 5, 3, 2, 1)}
        halo = [halo[0]] + [arrived[k] for k in range(1, n_dom)]
    else:
        halo = [lax.all_to_all(halo[0], "dom", split_axis=0, concat_axis=0, tiled=True)]
    near, mesh_encoded = call(
        near_edges_kernel,
        [shape_of((edges, hidden), F32), shape_of((mesh_rows, feats), BF16)],
        feat,
        full,
        send_proj,
        w_edge_recv,
        edge_bias[None, :],
        near_src,
        near_dst,
        specs=[SMEM] + [VMEM] * 6,
        name="near_edges",
    )
    proc_sum = call(
        edge_sums_kernel,
        shape_of((mesh_rows, hidden), BF16),
        near,
        far_src,
        into,
        *halo[::-1],
        scratch=[pltpu.VMEM((n_halo, hidden), BF16)],
        name="edge_sums",
    )
    part = call(
        own_output_kernel, shape_of((mesh_rows, feats), F32), mesh_encoded, proc_sum, w_out, name="own_output"
    )
    mesh_out = call(
        output_kernel, shape_of((mesh_rows, feats), BF16), part, swap(proc_sum), w_out, name="output"
    )
    return (mesh_encoded, mesh_out)


def solution(mesh):
    rows = P(("member", "dom"), "feat")
    columns, lists = P(None, "feat"), P("dom", None)
    placed = (rows, rows, columns, columns, P("feat"), P("feat", None), columns, columns, P("feat"), P("feat", None))
    return jax.shard_map(
        shards,
        mesh=mesh,
        in_specs=placed + (lists,) * 5,
        out_specs=(rows, rows),
        check_vma=False,
    )
```

```python
import functools

import jax
import jax.numpy as jnp
from jax import lax
from jax.experimental import pallas as pl
from jax.experimental.pallas import tpu as pltpu
from jax.sharding import PartitionSpec as P

BF16, F32, I32 = jnp.bfloat16, jnp.float32, jnp.int32
LANES = 128
STEP = 256
DIGIT = 64
MIB = 24
SMEM = pl.BlockSpec(memory_space=pltpu.SMEM)
VMEM = pl.BlockSpec(memory_space=pltpu.VMEM)
HBM = pl.BlockSpec(memory_space=pltpu.HBM)


def dot(a, b):
    return jnp.dot(a, b, preferred_element_type=F32)


def iota(shape, axis):
    return lax.broadcasted_iota(I32, shape, axis)


def silu_bf16(v):
    return (v / (1.0 + jnp.exp(-v))).astype(BF16)


def shape_of(shape, dtype):
    return jax.ShapeDtypeStruct(shape, dtype)


def position(axis):
    return lax.axis_index(axis).astype(I32).reshape(1)


def swap(x):
    return lax.ppermute(x, "feat", [(0, 1), (1, 0)])


def from_xor(x, bits, n_dom):
    return lax.ppermute(x, "dom", [(i, i ^ bits) for i in range(n_dom)])


def call(kernel, out_shape, *args, specs=None, outs=None, name, scratch=(), mib=MIB):
    return pl.pallas_call(
        kernel,
        out_shape=out_shape,
        in_specs=[VMEM] * len(args) if specs is None else specs,
        out_specs=jax.tree.map(lambda _: VMEM, out_shape) if outs is None else outs,
        scratch_shapes=scratch,
        compiler_params=pltpu.CompilerParams(vmem_limit_bytes=mib << 20),
        name=name,
    )(*args)


def halves_of(feat, size):
    own = pl.ds(pl.multiple_of(feat * size, size), size)
    other = pl.ds(pl.multiple_of((1 - feat) * size, size), size)
    return own, other


def start_copies(source, target, sems, first, pieces):
    rows = source.shape[0] // pieces
    copies = []
    for n in range(pieces):
        part = pl.ds(n * rows, rows)
        copies.append(pltpu.make_async_copy(source.at[part], target.at[part], sems.at[first + n]))
        copies[-1].start()
    return copies


def wait_copies(copies):
    for copy in copies:
        copy.wait()


def own_features_kernel(feat, grid, w_send, send, grid_part, send_rest, list_rows, digits, *scratch):
    ws, g, ids, sems = scratch
    copies = start_copies(send, ids, sems, 0, 1) + start_copies(w_send, ws, sems, 1, 4)
    copies += start_copies(grid, g, sems, 5, 8)
    own, other = halves_of(feat[0], g.shape[1])
    wait_copies(copies[:1])
    rows = jnp.concatenate([ids[:, a : a + LANES] for a in range(0, ids.shape[1], LANES)], axis=0)
    list_rows[...] = rows
    digits[...] = jnp.concatenate([rows // DIGIT, rows % DIGIT], axis=0).astype(F32).astype(BF16)
    wait_copies(copies[1:])
    grid_part[...] = dot(g[...], ws[own, :])
    send_rest[...] = ws[other, :]


def other_features_kernel(part, rest, other, *outs):
    width = outs[0].shape[1]
    for c, out in enumerate(outs):
        lanes = slice(c * width, (c + 1) * width)
        out[...] = (part[:, lanes] + dot(other[...], rest[:, lanes])).astype(BF16)


def with_list_kernel(part, rest, other, digits, *outs):
    *chunks, first = outs
    other_features_kernel(part, rest, other, *chunks)
    first[: part.shape[0], :] = chunks[0][...]
    first[part.shape[0] :, :] = digits[...]


def project(grid, w_send, send, n_chunks):
    grid_other = swap(grid)
    hidden, feats = w_send.shape[1], grid.shape[1]
    lines = send.shape[1] // LANES
    grid_part, send_rest, list_rows, digits = call(
        own_features_kernel,
        [
            shape_of((grid.shape[0], hidden), F32),
            shape_of((feats, hidden), BF16),
            shape_of((lines, LANES), I32),
            shape_of((2 * lines, LANES), BF16),
        ],
        position("feat"),
        *[pltpu.with_memory_space_constraint(x, pltpu.HBM) for x in (grid, w_send, send)],
        specs=[SMEM] + [HBM] * 3,
        scratch=[pltpu.VMEM(x.shape, x.dtype) for x in (w_send, grid, send)] + [pltpu.SemaphoreType.DMA((13,))],
        name="own_features",
    )
    chunk = shape_of((grid.shape[0], hidden // n_chunks), BF16)
    if n_chunks == 1:
        return call(
            other_features_kernel, [chunk], grid_part, send_rest, grid_other, name="other_grid_features"
        ), list_rows
    first = shape_of((grid.shape[0] + digits.shape[0], chunk.shape[1]), BF16)
    chunks = call(
        with_list_kernel,
        [chunk] * n_chunks + [first],
        grid_part,
        send_rest,
        grid_other,
        digits,
        name="other_grid_features",
    )
    return chunks, list_rows


def mesh_features_kernel(feat, mesh, other_mesh, w_recv, out):
    own, other = halves_of(feat[0], mesh.shape[1])
    out[...] = (dot(mesh[...], w_recv[own, :]) + dot(other_mesh[...], w_recv[other, :])).astype(BF16)


def project_mesh(mesh, mesh_other, w_recv):
    return call(
        mesh_features_kernel,
        shape_of((mesh.shape[0], w_recv.shape[1]), BF16),
        position("feat"),
        mesh,
        mesh_other,
        w_recv,
        specs=[SMEM] + [VMEM] * 3,
        name="mesh_features",
    )


def across(row):
    return jnp.transpose(jnp.broadcast_to(row.astype(F32), (LANES, LANES))).astype(I32)


def slots_of(ref, n, cap):
    return ref[:, pl.ds(pl.multiple_of(n * cap, cap), cap)]


def one_hot_rows(row, width, at):
    return (across(row[:, at : at + LANES])[:, :1] == iota((LANES, width), 1)).astype(BF16)


def pack_own_kernel(bits, me, list_rows, g0, g1, *outs):
    width, cap = g0.shape[1], outs[0].shape[0]
    for k, out in zip(bits, outs):
        for at in range(0, cap, LANES):
            ids = list_rows[pl.ds((me[0] ^ k) * (cap // LANES) + at // LANES, 1), :]
            hot = one_hot_rows(ids, g0.shape[0], 0)
            out[at : at + LANES, :width] = dot(hot, g0[...]).astype(BF16)
            out[at : at + LANES, width:] = dot(hot, g1[...]).astype(BF16)


def prepare_kernel(half, me, recv, mesh_proj, bias, into, term):
    cap = term.shape[0] // half
    for k in range(half):
        rows = slots_of(recv, me[0] ^ k ^ half, cap)
        first = k * cap
        into[:, first : first + cap] = (iota((into.shape[0], cap), 0) == rows).astype(BF16)
        for at in range(0, cap, LANES):
            here = slice(first + at, first + at + LANES)
            term[here, :] = dot(one_hot_rows(rows, mesh_proj.shape[0], at), mesh_proj[...]) + bias[...]


def aside_kernel(half, cap, blocks, me, list_rows, send, recv, g0, g1, mesh_proj, bias, halo_rows, src, dst, *outs):
    packed, sums, into, term, *selections = outs
    pack_own_kernel((1,), me, list_rows, g0, g1, packed)
    local_sums_kernel(cap, me, send, recv, g0, g1, mesh_proj, bias, sums)
    prepare_kernel(half, me, recv, mesh_proj, bias, into, term)
    select_kernel(blocks, me, halo_rows, src, dst, *selections)


def pick_kernel(half, me, mirrored, pick, ids):
    cap, grid_rows = pick.shape[0] // half, pick.shape[1]
    lines = ids.shape[0]
    digits = mirrored[grid_rows:, :].astype(F32).astype(I32)
    ids[...] = digits[:lines, :] * DIGIT + digits[lines:, :]
    for k in range(half):
        for n in range(cap // LANES):
            row = ids[pl.ds((me[0] ^ k) * (cap // LANES) + n, 1), :]
            first = k * cap + n * LANES
            pick[first : first + LANES, :] = one_hot_rows(row, grid_rows, 0)


def add_slots(total, grid, rows, mesh_proj, bias):
    hot = [one_hot_rows(rows, mesh_proj.shape[0], at) for at in range(0, rows.shape[1], LANES)]
    term = dot(jnp.concatenate(hot, axis=0), mesh_proj[...])
    into = (iota((mesh_proj.shape[0], rows.shape[1]), 0) == rows).astype(BF16)
    return total + dot(into, silu_bf16(grid + term + bias[...]))


def local_sums_kernel(cap, me, send, recv, g0, g1, mesh_proj, bias, out):
    ids, rows = slots_of(send, me[0], cap), slots_of(recv, me[0], cap)
    hot = jnp.concatenate([one_hot_rows(ids, g0.shape[0], at) for at in range(0, cap, LANES)], axis=0)
    grid = jnp.concatenate([dot(hot, g0[...]), dot(hot, g1[...])], axis=1)
    out[...] = add_slots(0.0, grid, rows, mesh_proj, bias)


def arrived_sums_kernel(cap, me, recv, mesh_proj, bias, start, *refs):
    *blocks, out = refs
    blocks.reverse()
    total = start[...]
    for k, block in enumerate(blocks, 1):
        total = add_slots(total, block[...].astype(F32), slots_of(recv, me[0] ^ k, cap), mesh_proj, bias)
    out[...] = total


def pack_mirror_kernel(pick, mirrored, *outs):
    cap = outs[0].shape[0]
    for k, out in enumerate(outs, 1):
        out[...] = dot(pick[k * cap : (k + 1) * cap, :], mirrored[: pick.shape[1], :]).astype(BF16)


def mirror_sums_kernel(chunk, first, pick, mirrored, into, term, total, *refs):
    *blocks, out = refs
    width = out.shape[1]
    lanes = slice(chunk * width, (chunk + 1) * width)
    cap = into.shape[1] // 4
    if first:
        blocks = [dot(pick[:cap, :], mirrored[: pick.shape[1], :])]
        sums = total[:, lanes]
    else:
        blocks.reverse()
        sums = total[...]
    for k, block in enumerate(blocks, 0 if first else 1):
        rows = slice(k * cap, (k + 1) * cap)
        hidden = silu_bf16(block[...].astype(F32) + term[rows, lanes])
        sums += dot(into[:, rows], hidden)
    out[...] = sums.astype(out.dtype)


def sums_by_halves(grid_chunks, list_rows, mesh, bias, send_grid, recv_row, n_dom, select, lists):
    half = n_dom // 2
    mesh_rows, hidden = mesh[0].shape[0], mesh[2].shape[1]
    *grid_chunks, with_list = grid_chunks
    grid_rows, width = grid_chunks[0].shape
    cap = send_grid.shape[1] // n_dom
    me, bias = position("dom"), bias[None, :]

    def pack_own(*bits):
        blocks = call(
            functools.partial(pack_own_kernel, bits),
            [shape_of((cap, hidden), BF16)] * len(bits),
            me,
            list_rows,
            *grid_chunks,
            specs=[SMEM] + [VMEM] * 3,
            name="pack_own",
        )
        return blocks

    packed = pack_own(3, 2)
    packed, with_list, grid_chunks, mesh = lax.optimization_barrier((packed, with_list, grid_chunks, mesh))
    mesh_rproj = project_mesh(*mesh)
    arrived = {k: from_xor(block, k, n_dom) for k, block in zip((3, 2), packed)}
    mirrored = [from_xor(with_list, half, n_dom)]
    selection_shapes, blocks = select
    packed, own, into, term, *selections = call(
        functools.partial(aside_kernel, half, cap, blocks),
        [
            shape_of((cap, hidden), BF16),
            shape_of((mesh_rows, hidden), F32),
            shape_of((mesh_rows, half * cap), BF16),
            shape_of((half * cap, hidden), F32),
            *selection_shapes,
        ],
        me,
        list_rows,
        send_grid,
        recv_row,
        *grid_chunks,
        mesh_rproj,
        bias,
        *lists,
        specs=[SMEM] + [VMEM] * (7 + len(lists)),
        name="aside",
    )
    arrived[1] = from_xor(packed, 1, n_dom)
    arrived = [arrived[k] for k in range(1, half)]
    mirrored.append(from_xor(grid_chunks[1], half, n_dom))
    own, into, term, selections, mirrored[0] = lax.optimization_barrier((own, into, term, selections, mirrored[0]))
    pick = call(
        functools.partial(pick_kernel, half),
        shape_of((half * cap, grid_rows), BF16),
        me,
        mirrored[0],
        specs=[SMEM, VMEM],
        scratch=[pltpu.VMEM((send_grid.shape[1] // LANES, LANES), I32)],
        name="pick",
    )
    own = call(
        functools.partial(arrived_sums_kernel, cap),
        shape_of((mesh_rows, hidden), F32),
        me,
        recv_row,
        mesh_rproj,
        bias,
        own,
        *arrived[::-1],
        specs=[SMEM] + [VMEM] * (4 + len(arrived)),
        name="arrived_sums",
    )
    chunks = []
    for c in range(2):
        blocks = call(
            pack_mirror_kernel, [shape_of((cap, width), BF16)] * (half - 1), pick, mirrored[c], name="pack_mirror"
        )
        blocks = [from_xor(block, k, n_dom) for k, block in enumerate(blocks, 1)]
        total = call(
            functools.partial(mirror_sums_kernel, c, True),
            shape_of((mesh_rows, width), F32),
            pick,
            mirrored[c],
            into,
            term,
            own,
            name="own_mirror_sums",
        )
        chunks.append(
            call(
                functools.partial(mirror_sums_kernel, c, False),
                shape_of((mesh_rows, width), BF16),
                pick,
                mirrored[c],
                into,
                term,
                total,
                *blocks[::-1],
                name="mirror_sums",
            )
        )
    return chunks, selections


def sums_by_all_to_all(grid_chunks, list_rows, mesh, bias, send_grid, recv_row, n_dom, select, lists):
    mesh_rproj = project_mesh(*mesh)

    def rows_of(table, index):
        hot = index[0][:, None] == iota((index.shape[1], table.shape[0]), 1)
        return dot(hot.astype(BF16), table)

    packed = rows_of(grid_chunks[0], send_grid).astype(BF16)
    arrived = lax.all_to_all(packed, "dom", split_axis=0, concat_axis=0, tiled=True)
    hidden = silu_bf16(arrived.astype(F32) + rows_of(mesh_rproj, recv_row) + bias[None, :])
    into = iota((mesh_rproj.shape[0], recv_row.shape[1]), 0) == recv_row
    selection_shapes, blocks = select
    selections = call(
        functools.partial(select_kernel, blocks),
        selection_shapes,
        position("dom"),
        *lists,
        specs=[SMEM] + [VMEM] * len(lists),
        name="select",
    )
    return [dot(into.astype(BF16), hidden).astype(BF16)], selections


def list_rows(ref, me, k, blocks):
    size = ref.shape[1] // blocks
    return slots_of(ref, me ^ k, size) if blocks > 1 else ref[...]


def select_kernel(blocks, me, halo_rows, src, dst, halo_pick, near_src, near_dst, far_src, into):
    mesh_rows = into.shape[0]
    size = halo_pick.shape[0] // blocks
    for k in range(blocks):
        rows = list_rows(halo_rows, me[0], k, blocks)
        for a in range(0, size, LANES):
            halo_pick[k * size + a : k * size + a + LANES, :] = one_hot_rows(rows, mesh_rows, a)
    for b in range(src.shape[0]):
        rows = slice(b * LANES, (b + 1) * LANES)
        senders, receivers = src[b : b + 1, :], dst[b : b + 1, :]
        far = senders - mesh_rows
        if blocks > 1:
            far = jnp.where(far < 0, far, ((far // size) ^ me[0]) * size + far % size)
        near_src[rows, :] = one_hot_rows(senders, mesh_rows, 0)
        near_dst[rows, :] = one_hot_rows(receivers, mesh_rows, 0)
        far_src[rows, :] = one_hot_rows(far, far_src.shape[1], 0)
        into[:, rows] = (iota((mesh_rows, LANES), 0) == receivers).astype(BF16)


def encode_base_kernel(n_chunks, feat, *refs):
    chunks, others = refs[:n_chunks], refs[n_chunks : 2 * n_chunks]
    mesh_own, mesh_other, w_own, w_other, w2_own, w2_other, base, w2 = refs[2 * n_chunks :]
    feats = mesh_own.shape[1]
    own, rest = halves_of(feat[0], feats)
    base[:, own] = mesh_own[...].astype(F32)
    base[:, rest] = mesh_other[...].astype(F32)
    at = 0
    for mine, other in zip(chunks, others):
        rows = slice(at, at + mine.shape[1])
        base[...] += dot(mine[...], w_own[rows, :]) + dot(other[...], w_other[rows, :])
        at += mine.shape[1]
    w2[: w2_own.shape[0], :] = w2_own[:, own]
    w2[w2_own.shape[0] :, :] = w2_other[:, own]


def encode_kernel(first, base, mine, other, w_own, w_other, w_send, pick, full, send_proj, *halo):
    rows = slice(first, first + mine.shape[1])
    full[...] = (base[...] + dot(mine[...], w_own[rows, :]) + dot(other[...], w_other[rows, :])).astype(BF16)
    send_proj[...] = dot(full[...], w_send[...]).astype(BF16)
    size = halo[0].shape[0]
    for k, out in enumerate(halo):
        out[...] = dot(pick[k * size : (k + 1) * size, :], send_proj[...]).astype(BF16)


def near_edges_kernel(feat, full, send_proj, w_recv, bias, near_src, near_dst, near, encoded):
    own, _ = halves_of(feat[0], encoded.shape[1])
    encoded[...] = full[:, own]
    recv_proj = dot(full[...], w_recv[...]).astype(BF16)
    for at in range(0, near.shape[0], STEP):
        rows = slice(at, at + STEP)
        near[rows, :] = dot(near_src[rows, :], send_proj[...]) + dot(near_dst[rows, :], recv_proj) + bias[...]


def edge_sums_kernel(near, far_pick, into, *refs):
    *halo, out, table = refs
    halo.reverse()
    size = halo[0].shape[0]
    for k, block in enumerate(halo):
        table[k * size : (k + 1) * size, :] = block[...]
    total = jnp.zeros(out.shape, F32)
    for at in range(0, near.shape[0], STEP):
        rows = slice(at, at + STEP)
        hidden = silu_bf16(near[rows, :] + dot(far_pick[rows, :], table[...]))
        total += dot(into[:, rows], hidden)
    out[...] = total.astype(BF16)


def own_output_kernel(encoded, mine, w_out, out):
    out[...] = encoded[...].astype(F32) + dot(mine[...], w_out[: mine.shape[1], :])


def output_kernel(part, other, w_out, out):
    out[...] = (part[...] + dot(other[...], w_out[other.shape[1] :, :])).astype(BF16)


def shards(
    grid_lat,
    mesh_lat,
    w_grid_send,
    w_grid_recv,
    g2m_bias,
    w_grid_out,
    w_edge_send,
    w_edge_recv,
    edge_bias,
    w_edge_out,
    send_grid,
    recv_row,
    halo_rows,
    edge_src,
    edge_dst,
):
    n_dom = lax.axis_size("dom")
    mesh_rows, feats = mesh_lat.shape
    hidden = w_grid_send.shape[1]
    halves = n_dom == 8
    grid_chunks, list_rows = project(grid_lat, w_grid_send, send_grid, 2 if halves else 1)
    grid_chunks, list_rows, send_grid, recv_row, mesh_lat, mesh_other, w_other, w2_other = lax.optimization_barrier(
        (grid_chunks, list_rows, send_grid, recv_row, mesh_lat, swap(mesh_lat), swap(w_grid_out), swap(w_edge_out))
    )
    mesh = (mesh_lat, mesh_other, w_grid_recv)
    me, feat = position("dom"), position("feat")
    blocks = n_dom if halves else 1
    n_halo, edges = halo_rows.shape[1], edge_src.shape[0] * edge_src.shape[1]
    select = (
        [
            shape_of((n_halo, mesh_rows), BF16),
            shape_of((edges, mesh_rows), BF16),
            shape_of((edges, mesh_rows), BF16),
            shape_of((edges, n_halo), BF16),
            shape_of((mesh_rows, edges), BF16),
        ],
        blocks,
    )
    sums = sums_by_halves if halves else sums_by_all_to_all
    lists = (halo_rows, edge_src, edge_dst)
    chunks, selections = sums(grid_chunks, list_rows, mesh, g2m_bias, send_grid, recv_row, n_dom, select, lists)
    pick, near_src, near_dst, far_src, into = selections
    *early, last = chunks
    base, w_out = call(
        functools.partial(encode_base_kernel, len(early)),
        [shape_of((mesh_rows, 2 * feats), F32), shape_of((2 * w_edge_out.shape[0], feats), BF16)],
        feat,
        *early,
        *[swap(chunk) for chunk in early],
        mesh_lat,
        mesh_other,
        w_grid_out,
        w_other,
        w_edge_out,
        w2_other,
        specs=[SMEM] + [VMEM] * (2 * len(early) + 6),
        name="encode_base",
    )
    full, send_proj, *halo = call(
        functools.partial(encode_kernel, hidden - last.shape[1]),
        [shape_of((mesh_rows, 2 * feats), BF16), shape_of((mesh_rows, hidden), BF16)]
        + [shape_of((n_halo // blocks, hidden), BF16)] * blocks,
        base,
        last,
        swap(last),
        w_grid_out,
        w_other,
        w_edge_send,
        pick,
        name="encode",
    )
    if halves:
        arrived = {k: from_xor(halo[k], k, n_dom) for k in (6, 7, 4, 5, 3, 2, 1)}
        halo = [halo[0]] + [arrived[k] for k in range(1, n_dom)]
    else:
        halo = [lax.all_to_all(halo[0], "dom", split_axis=0, concat_axis=0, tiled=True)]
    near, mesh_encoded = call(
        near_edges_kernel,
        [shape_of((edges, hidden), F32), shape_of((mesh_rows, feats), BF16)],
        feat,
        full,
        send_proj,
        w_edge_recv,
        edge_bias[None, :],
        near_src,
        near_dst,
        specs=[SMEM] + [VMEM] * 6,
        name="near_edges",
    )
    proc_sum = call(
        edge_sums_kernel,
        shape_of((mesh_rows, hidden), BF16),
        near,
        far_src,
        into,
        *halo[::-1],
        scratch=[pltpu.VMEM((n_halo, hidden), BF16)],
        name="edge_sums",
    )
    part = call(
        own_output_kernel, shape_of((mesh_rows, feats), F32), mesh_encoded, proc_sum, w_out, name="own_output"
    )
    mesh_out = call(
        output_kernel, shape_of((mesh_rows, feats), BF16), part, swap(proc_sum), w_out, name="output"
    )
    return (mesh_encoded, mesh_out)


def solution(mesh):
    rows = P(("member", "dom"), "feat")
    columns, lists = P(None, "feat"), P("dom", None)
    placed = (rows, rows, columns, columns, P("feat"), P("feat", None), columns, columns, P("feat"), P("feat", None))
    return jax.shard_map(
        shards,
        mesh=mesh,
        in_specs=placed + (lists,) * 5,
        out_specs=(rows, rows),
        check_vma=False,
    )
```

```python
import functools

import jax
import jax.numpy as jnp
from jax import lax
from jax.experimental import pallas as pl
from jax.experimental.pallas import tpu as pltpu
from jax.sharding import PartitionSpec as P

BF16, F32, I32 = jnp.bfloat16, jnp.float32, jnp.int32
LANES = 128
STEP = 256
DIGIT = 64
MIB = 24
SMEM = pl.BlockSpec(memory_space=pltpu.SMEM)
VMEM = pl.BlockSpec(memory_space=pltpu.VMEM)
HBM = pl.BlockSpec(memory_space=pltpu.HBM)


def dot(a, b):
    return jnp.dot(a, b, preferred_element_type=F32)


def iota(shape, axis):
    return lax.broadcasted_iota(I32, shape, axis)


def silu_bf16(v):
    return (v / (1.0 + jnp.exp(-v))).astype(BF16)


def shape_of(shape, dtype):
    return jax.ShapeDtypeStruct(shape, dtype)


def position(axis):
    return lax.axis_index(axis).astype(I32).reshape(1)


def swap(x):
    return lax.ppermute(x, "feat", [(0, 1), (1, 0)])


def from_xor(x, bits, n_dom):
    return lax.ppermute(x, "dom", [(i, i ^ bits) for i in range(n_dom)])


def call(kernel, out_shape, *args, specs=None, outs=None, name, scratch=(), mib=MIB):
    return pl.pallas_call(
        kernel,
        out_shape=out_shape,
        in_specs=[VMEM] * len(args) if specs is None else specs,
        out_specs=jax.tree.map(lambda _: VMEM, out_shape) if outs is None else outs,
        scratch_shapes=scratch,
        compiler_params=pltpu.CompilerParams(vmem_limit_bytes=mib << 20),
        name=name,
    )(*args)


def halves_of(feat, size):
    own = pl.ds(pl.multiple_of(feat * size, size), size)
    other = pl.ds(pl.multiple_of((1 - feat) * size, size), size)
    return own, other


def start_copies(source, target, sems, first, pieces):
    rows = source.shape[0] // pieces
    copies = []
    for n in range(pieces):
        part = pl.ds(n * rows, rows)
        copies.append(pltpu.make_async_copy(source.at[part], target.at[part], sems.at[first + n]))
        copies[-1].start()
    return copies


def wait_copies(copies):
    for copy in copies:
        copy.wait()


def own_features_kernel(feat, grid, w_send, send, grid_part, send_rest, list_rows, digits, *scratch):
    ws, g, ids, sems = scratch
    copies = start_copies(send, ids, sems, 0, 1) + start_copies(w_send, ws, sems, 1, 4)
    copies += start_copies(grid, g, sems, 5, 8)
    own, other = halves_of(feat[0], g.shape[1])
    wait_copies(copies[:1])
    rows = jnp.concatenate([ids[:, a : a + LANES] for a in range(0, ids.shape[1], LANES)], axis=0)
    list_rows[...] = rows
    digits[...] = jnp.concatenate([rows // DIGIT, rows % DIGIT], axis=0).astype(F32).astype(BF16)
    wait_copies(copies[1:])
    grid_part[...] = dot(g[...], ws[own, :])
    send_rest[...] = ws[other, :]


def other_features_kernel(part, rest, other, *outs):
    width = outs[0].shape[1]
    for c, out in enumerate(outs):
        lanes = slice(c * width, (c + 1) * width)
        out[...] = (part[:, lanes] + dot(other[...], rest[:, lanes])).astype(BF16)


def with_list_kernel(part, rest, other, digits, *outs):
    *chunks, first = outs
    other_features_kernel(part, rest, other, *chunks)
    first[: part.shape[0], :] = chunks[0][...]
    first[part.shape[0] :, :] = digits[...]


def project(grid, w_send, send, n_chunks):
    grid_other = swap(grid)
    hidden, feats = w_send.shape[1], grid.shape[1]
    lines = send.shape[1] // LANES
    grid_part, send_rest, list_rows, digits = call(
        own_features_kernel,
        [
            shape_of((grid.shape[0], hidden), F32),
            shape_of((feats, hidden), BF16),
            shape_of((lines, LANES), I32),
            shape_of((2 * lines, LANES), BF16),
        ],
        position("feat"),
        *[pltpu.with_memory_space_constraint(x, pltpu.HBM) for x in (grid, w_send, send)],
        specs=[SMEM] + [HBM] * 3,
        scratch=[pltpu.VMEM(x.shape, x.dtype) for x in (w_send, grid, send)] + [pltpu.SemaphoreType.DMA((13,))],
        name="own_features",
    )
    chunk = shape_of((grid.shape[0], hidden // n_chunks), BF16)
    if n_chunks == 1:
        return call(
            other_features_kernel, [chunk], grid_part, send_rest, grid_other, name="other_grid_features"
        ), list_rows
    first = shape_of((grid.shape[0] + digits.shape[0], chunk.shape[1]), BF16)
    chunks = call(
        with_list_kernel,
        [chunk] * n_chunks + [first],
        grid_part,
        send_rest,
        grid_other,
        digits,
        name="other_grid_features",
    )
    return chunks, list_rows


def mesh_features_kernel(feat, mesh, other_mesh, w_recv, out):
    own, other = halves_of(feat[0], mesh.shape[1])
    out[...] = (dot(mesh[...], w_recv[own, :]) + dot(other_mesh[...], w_recv[other, :])).astype(BF16)


def project_mesh(mesh, mesh_other, w_recv):
    return call(
        mesh_features_kernel,
        shape_of((mesh.shape[0], w_recv.shape[1]), BF16),
        position("feat"),
        mesh,
        mesh_other,
        w_recv,
        specs=[SMEM] + [VMEM] * 3,
        name="mesh_features",
    )


def across(row):
    return jnp.transpose(jnp.broadcast_to(row.astype(F32), (LANES, LANES))).astype(I32)


def slots_of(ref, n, cap):
    return ref[:, pl.ds(pl.multiple_of(n * cap, cap), cap)]


def one_hot_rows(row, width, at):
    return (across(row[:, at : at + LANES])[:, :1] == iota((LANES, width), 1)).astype(BF16)


def pack_own_kernel(bits, me, list_rows, g0, g1, *outs):
    width, cap = g0.shape[1], outs[0].shape[0]
    for k, out in zip(bits, outs):
        for at in range(0, cap, LANES):
            ids = list_rows[pl.ds((me[0] ^ k) * (cap // LANES) + at // LANES, 1), :]
            hot = one_hot_rows(ids, g0.shape[0], 0)
            out[at : at + LANES, :width] = dot(hot, g0[...]).astype(BF16)
            out[at : at + LANES, width:] = dot(hot, g1[...]).astype(BF16)


def prepare_kernel(half, bits, me, recv, mesh_proj, bias, into, term):
    cap = term.shape[0] // len(bits)
    for n, k in enumerate(bits):
        rows = slots_of(recv, me[0] ^ k, cap)
        first = n * cap
        into[:, first : first + cap] = (iota((into.shape[0], cap), 0) == rows).astype(BF16)
        for at in range(0, cap, LANES):
            here = slice(first + at, first + at + LANES)
            term[here, :] = dot(one_hot_rows(rows, mesh_proj.shape[0], at), mesh_proj[...]) + bias[...]


def aside_kernel(half, cap, blocks, me, list_rows, send, recv, g0, g1, mesh_proj, bias, halo_rows, src, dst, *outs):
    packed, sums, into, term, *selections = outs
    pack_own_kernel((1,), me, list_rows, g0, g1, packed)
    local_sums_kernel(cap, me, send, recv, g0, g1, mesh_proj, bias, sums)
    prepare_kernel(half, slot_order(half), me, recv, mesh_proj, bias, into, term)
    select_kernel(blocks, me, halo_rows, src, dst, *selections)


def slot_order(half):
    return [k ^ half for k in range(half)] + list(range(1, half))


def pick_kernel(half, me, mirrored, pick, ids):
    cap, grid_rows = pick.shape[0] // half, pick.shape[1]
    lines = ids.shape[0]
    digits = mirrored[grid_rows:, :].astype(F32).astype(I32)
    ids[...] = digits[:lines, :] * DIGIT + digits[lines:, :]
    for k in range(half):
        for n in range(cap // LANES):
            row = ids[pl.ds((me[0] ^ k) * (cap // LANES) + n, 1), :]
            first = k * cap + n * LANES
            pick[first : first + LANES, :] = one_hot_rows(row, grid_rows, 0)


def add_slots(total, grid, rows, mesh_proj, bias):
    hot = [one_hot_rows(rows, mesh_proj.shape[0], at) for at in range(0, rows.shape[1], LANES)]
    term = dot(jnp.concatenate(hot, axis=0), mesh_proj[...])
    into = (iota((mesh_proj.shape[0], rows.shape[1]), 0) == rows).astype(BF16)
    return total + dot(into, silu_bf16(grid + term + bias[...]))


def local_sums_kernel(cap, me, send, recv, g0, g1, mesh_proj, bias, out):
    ids, rows = slots_of(send, me[0], cap), slots_of(recv, me[0], cap)
    hot = jnp.concatenate([one_hot_rows(ids, g0.shape[0], at) for at in range(0, cap, LANES)], axis=0)
    grid = jnp.concatenate([dot(hot, g0[...]), dot(hot, g1[...])], axis=1)
    out[...] = add_slots(0.0, grid, rows, mesh_proj, bias)


def arrived_sums_kernel(first, into, term, *refs):
    *blocks, out = refs
    blocks.reverse()
    cap = blocks[0].shape[0]
    total = 0.0
    for k, block in enumerate(blocks):
        rows = slice(first + k * cap, first + (k + 1) * cap)
        total += dot(into[:, rows], silu_bf16(block[...].astype(F32) + term[rows, :]))
    out[...] = total


def pack_mirror_kernel(pick, mirrored, *outs):
    cap = outs[0].shape[0]
    for k, out in enumerate(outs, 1):
        out[...] = dot(pick[k * cap : (k + 1) * cap, :], mirrored[: pick.shape[1], :]).astype(BF16)


def own_mirror_sums_kernel(chunk, pick, mirrored, into, term, own, out):
    width, cap = out.shape[1], pick.shape[0] // 4
    lanes = slice(chunk * width, (chunk + 1) * width)
    grid = dot(pick[:cap, :], mirrored[: pick.shape[1], :])
    out[...] = own[:, lanes] + dot(into[:, :cap], silu_bf16(grid + term[:cap, lanes]))


def mirror_sums_kernel(chunk, into, term, total, arrived, *refs):
    *blocks, out = refs
    blocks.reverse()
    width, cap = out.shape[1], blocks[0].shape[0]
    lanes = slice(chunk * width, (chunk + 1) * width)
    sums = total[...] + arrived[:, lanes]
    for k, block in enumerate(blocks, 1):
        rows = slice(k * cap, (k + 1) * cap)
        sums += dot(into[:, rows], silu_bf16(block[...].astype(F32) + term[rows, lanes]))
    out[...] = sums.astype(out.dtype)


def sums_by_halves(grid_chunks, list_rows, mesh, bias, send_grid, recv_row, n_dom, select, lists):
    half = n_dom // 2
    mesh_rows, hidden = mesh[0].shape[0], mesh[2].shape[1]
    *grid_chunks, with_list = grid_chunks
    grid_rows, width = grid_chunks[0].shape
    cap = send_grid.shape[1] // n_dom
    me, bias = position("dom"), bias[None, :]

    def pack_own(*bits):
        blocks = call(
            functools.partial(pack_own_kernel, bits),
            [shape_of((cap, hidden), BF16)] * len(bits),
            me,
            list_rows,
            *grid_chunks,
            specs=[SMEM] + [VMEM] * 3,
            name="pack_own",
        )
        return blocks

    packed = pack_own(3, 2)
    packed, with_list, grid_chunks, mesh = lax.optimization_barrier((packed, with_list, grid_chunks, mesh))
    mesh_rproj = project_mesh(*mesh)
    arrived = {k: from_xor(block, k, n_dom) for k, block in zip((3, 2), packed)}
    mirrored = [from_xor(with_list, half, n_dom)]
    selection_shapes, blocks = select
    packed, own, into, term, *selections = call(
        functools.partial(aside_kernel, half, cap, blocks),
        [
            shape_of((cap, hidden), BF16),
            shape_of((mesh_rows, hidden), F32),
            shape_of((mesh_rows, len(slot_order(half)) * cap), BF16),
            shape_of((len(slot_order(half)) * cap, hidden), F32),
            *selection_shapes,
        ],
        me,
        list_rows,
        send_grid,
        recv_row,
        *grid_chunks,
        mesh_rproj,
        bias,
        *lists,
        specs=[SMEM] + [VMEM] * (7 + len(lists)),
        name="aside",
    )
    arrived[1] = from_xor(packed, 1, n_dom)
    arrived = [arrived[k] for k in range(1, half)]
    mirrored.append(from_xor(grid_chunks[1], half, n_dom))
    own, into, term, selections, mirrored[0] = lax.optimization_barrier((own, into, term, selections, mirrored[0]))
    pick = call(
        functools.partial(pick_kernel, half),
        shape_of((half * cap, grid_rows), BF16),
        me,
        mirrored[0],
        specs=[SMEM, VMEM],
        scratch=[pltpu.VMEM((send_grid.shape[1] // LANES, LANES), I32)],
        name="pick",
    )
    from_half = call(
        functools.partial(arrived_sums_kernel, half * cap),
        shape_of((mesh_rows, hidden), F32),
        into,
        term,
        *arrived[::-1],
        name="arrived_sums",
    )
    chunks = []
    for c in range(2):
        blocks = call(
            pack_mirror_kernel, [shape_of((cap, width), BF16)] * (half - 1), pick, mirrored[c], name="pack_mirror"
        )
        blocks = [from_xor(block, k, n_dom) for k, block in enumerate(blocks, 1)]
        total = call(
            functools.partial(own_mirror_sums_kernel, c),
            shape_of((mesh_rows, width), F32),
            pick,
            mirrored[c],
            into,
            term,
            own,
            name="own_mirror_sums",
        )
        chunks.append(
            call(
                functools.partial(mirror_sums_kernel, c),
                shape_of((mesh_rows, width), BF16),
                into,
                term,
                total,
                from_half,
                *blocks[::-1],
                name="mirror_sums",
            )
        )
    return chunks, selections


def sums_by_all_to_all(grid_chunks, list_rows, mesh, bias, send_grid, recv_row, n_dom, select, lists):
    mesh_rproj = project_mesh(*mesh)

    def rows_of(table, index):
        hot = index[0][:, None] == iota((index.shape[1], table.shape[0]), 1)
        return dot(hot.astype(BF16), table)

    packed = rows_of(grid_chunks[0], send_grid).astype(BF16)
    arrived = lax.all_to_all(packed, "dom", split_axis=0, concat_axis=0, tiled=True)
    hidden = silu_bf16(arrived.astype(F32) + rows_of(mesh_rproj, recv_row) + bias[None, :])
    into = iota((mesh_rproj.shape[0], recv_row.shape[1]), 0) == recv_row
    selection_shapes, blocks = select
    selections = call(
        functools.partial(select_kernel, blocks),
        selection_shapes,
        position("dom"),
        *lists,
        specs=[SMEM] + [VMEM] * len(lists),
        name="select",
    )
    return [dot(into.astype(BF16), hidden).astype(BF16)], selections


def list_rows(ref, me, k, blocks):
    size = ref.shape[1] // blocks
    return slots_of(ref, me ^ k, size) if blocks > 1 else ref[...]


def select_kernel(blocks, me, halo_rows, src, dst, halo_pick, near_src, near_dst, far_src, into):
    mesh_rows = into.shape[0]
    size = halo_pick.shape[0] // blocks
    for k in range(blocks):
        rows = list_rows(halo_rows, me[0], k, blocks)
        for a in range(0, size, LANES):
            halo_pick[k * size + a : k * size + a + LANES, :] = one_hot_rows(rows, mesh_rows, a)
    for b in range(src.shape[0]):
        rows = slice(b * LANES, (b + 1) * LANES)
        senders, receivers = src[b : b + 1, :], dst[b : b + 1, :]
        far = senders - mesh_rows
        if blocks > 1:
            far = jnp.where(far < 0, far, ((far // size) ^ me[0]) * size + far % size)
        near_src[rows, :] = one_hot_rows(senders, mesh_rows, 0)
        near_dst[rows, :] = one_hot_rows(receivers, mesh_rows, 0)
        far_src[rows, :] = one_hot_rows(far, far_src.shape[1], 0)
        into[:, rows] = (iota((mesh_rows, LANES), 0) == receivers).astype(BF16)


def encode_base_kernel(n_chunks, feat, *refs):
    chunks, others = refs[:n_chunks], refs[n_chunks : 2 * n_chunks]
    mesh_own, mesh_other, w_own, w_other, w2_own, w2_other, base, w2 = refs[2 * n_chunks :]
    feats = mesh_own.shape[1]
    own, rest = halves_of(feat[0], feats)
    base[:, own] = mesh_own[...].astype(F32)
    base[:, rest] = mesh_other[...].astype(F32)
    at = 0
    for mine, other in zip(chunks, others):
        rows = slice(at, at + mine.shape[1])
        base[...] += dot(mine[...], w_own[rows, :]) + dot(other[...], w_other[rows, :])
        at += mine.shape[1]
    w2[: w2_own.shape[0], :] = w2_own[:, own]
    w2[w2_own.shape[0] :, :] = w2_other[:, own]


def encode_kernel(first, base, mine, other, w_own, w_other, w_send, pick, full, send_proj, *halo):
    rows = slice(first, first + mine.shape[1])
    full[...] = (base[...] + dot(mine[...], w_own[rows, :]) + dot(other[...], w_other[rows, :])).astype(BF16)
    send_proj[...] = dot(full[...], w_send[...]).astype(BF16)
    size = halo[0].shape[0]
    for k, out in enumerate(halo):
        out[...] = dot(pick[k * size : (k + 1) * size, :], send_proj[...]).astype(BF16)


def near_edges_kernel(feat, full, send_proj, w_recv, bias, near_src, near_dst, near, encoded):
    own, _ = halves_of(feat[0], encoded.shape[1])
    encoded[...] = full[:, own]
    recv_proj = dot(full[...], w_recv[...]).astype(BF16)
    for at in range(0, near.shape[0], STEP):
        rows = slice(at, at + STEP)
        near[rows, :] = dot(near_src[rows, :], send_proj[...]) + dot(near_dst[rows, :], recv_proj) + bias[...]


def edge_sums_kernel(near, far_pick, into, *refs):
    *halo, out, table = refs
    halo.reverse()
    size = halo[0].shape[0]
    for k, block in enumerate(halo):
        table[k * size : (k + 1) * size, :] = block[...]
    total = jnp.zeros(out.shape, F32)
    for at in range(0, near.shape[0], STEP):
        rows = slice(at, at + STEP)
        hidden = silu_bf16(near[rows, :] + dot(far_pick[rows, :], table[...]))
        total += dot(into[:, rows], hidden)
    out[...] = total.astype(BF16)


def own_output_kernel(encoded, mine, w_out, out):
    out[...] = encoded[...].astype(F32) + dot(mine[...], w_out[: mine.shape[1], :])


def output_kernel(part, other, w_out, out):
    out[...] = (part[...] + dot(other[...], w_out[other.shape[1] :, :])).astype(BF16)


def shards(
    grid_lat,
    mesh_lat,
    w_grid_send,
    w_grid_recv,
    g2m_bias,
    w_grid_out,
    w_edge_send,
    w_edge_recv,
    edge_bias,
    w_edge_out,
    send_grid,
    recv_row,
    halo_rows,
    edge_src,
    edge_dst,
):
    n_dom = lax.axis_size("dom")
    mesh_rows, feats = mesh_lat.shape
    hidden = w_grid_send.shape[1]
    halves = n_dom == 8
    grid_chunks, list_rows = project(grid_lat, w_grid_send, send_grid, 2 if halves else 1)
    grid_chunks, list_rows, send_grid, recv_row, mesh_lat, mesh_other = lax.optimization_barrier(
        (grid_chunks, list_rows, send_grid, recv_row, mesh_lat, swap(mesh_lat))
    )
    mesh = (mesh_lat, mesh_other, w_grid_recv)
    me, feat = position("dom"), position("feat")
    blocks = n_dom if halves else 1
    n_halo, edges = halo_rows.shape[1], edge_src.shape[0] * edge_src.shape[1]
    select = (
        [
            shape_of((n_halo, mesh_rows), BF16),
            shape_of((edges, mesh_rows), BF16),
            shape_of((edges, mesh_rows), BF16),
            shape_of((edges, n_halo), BF16),
            shape_of((mesh_rows, edges), BF16),
        ],
        blocks,
    )
    sums = sums_by_halves if halves else sums_by_all_to_all
    lists = (halo_rows, edge_src, edge_dst)
    chunks, selections = sums(grid_chunks, list_rows, mesh, g2m_bias, send_grid, recv_row, n_dom, select, lists)
    selections, w_grid_out, w_edge_out = lax.optimization_barrier((selections, w_grid_out, w_edge_out))
    w_other, w2_other = swap(w_grid_out), swap(w_edge_out)
    pick, near_src, near_dst, far_src, into = selections
    *early, last = chunks
    base, w_out = call(
        functools.partial(encode_base_kernel, len(early)),
        [shape_of((mesh_rows, 2 * feats), F32), shape_of((2 * w_edge_out.shape[0], feats), BF16)],
        feat,
        *early,
        *[swap(chunk) for chunk in early],
        mesh_lat,
        mesh_other,
        w_grid_out,
        w_other,
        w_edge_out,
        w2_other,
        specs=[SMEM] + [VMEM] * (2 * len(early) + 6),
        name="encode_base",
    )
    full, send_proj, *halo = call(
        functools.partial(encode_kernel, hidden - last.shape[1]),
        [shape_of((mesh_rows, 2 * feats), BF16), shape_of((mesh_rows, hidden), BF16)]
        + [shape_of((n_halo // blocks, hidden), BF16)] * blocks,
        base,
        last,
        swap(last),
        w_grid_out,
        w_other,
        w_edge_send,
        pick,
        name="encode",
    )
    if halves:
        arrived = {k: from_xor(halo[k], k, n_dom) for k in (6, 7, 4, 5, 3, 2, 1)}
        halo = [halo[0]] + [arrived[k] for k in range(1, n_dom)]
    else:
        halo = [lax.all_to_all(halo[0], "dom", split_axis=0, concat_axis=0, tiled=True)]
    near, mesh_encoded = call(
        near_edges_kernel,
        [shape_of((edges, hidden), F32), shape_of((mesh_rows, feats), BF16)],
        feat,
        full,
        send_proj,
        w_edge_recv,
        edge_bias[None, :],
        near_src,
        near_dst,
        specs=[SMEM] + [VMEM] * 6,
        name="near_edges",
    )
    proc_sum = call(
        edge_sums_kernel,
        shape_of((mesh_rows, hidden), BF16),
        near,
        far_src,
        into,
        *halo[::-1],
        scratch=[pltpu.VMEM((n_halo, hidden), BF16)],
        name="edge_sums",
    )
    part = call(
        own_output_kernel, shape_of((mesh_rows, feats), F32), mesh_encoded, proc_sum, w_out, name="own_output"
    )
    mesh_out = call(
        output_kernel, shape_of((mesh_rows, feats), BF16), part, swap(proc_sum), w_out, name="output"
    )
    return (mesh_encoded, mesh_out)


def solution(mesh):
    rows = P(("member", "dom"), "feat")
    columns, lists = P(None, "feat"), P("dom", None)
    placed = (rows, rows, columns, columns, P("feat"), P("feat", None), columns, columns, P("feat"), P("feat", None))
    return jax.shard_map(
        shards,
        mesh=mesh,
        in_specs=placed + (lists,) * 5,
        out_specs=(rows, rows),
        check_vma=False,
    )
```
